512 devices in a mesh: dp: 16 (over x_lo, y), fsdp: 32 (over z, x_hi, core).
Axes of the slice: x: 4 (x_hi: 2, x_lo: 2; x = x_hi * 2 + x_lo), y: 8, z: 8, core: 2. Of those that a mesh axis runs over, the one named last changes fastest.
Arguments:
- acts: bfloat16 [8192, 32768], P('fsdp', 'dp'), may hold values from -6 to 6
- grads: bfloat16 [32768, 14336], P('dp', 'fsdp'), may hold values from -0.01953125 to 0.01953125
- basis: bfloat16 [8192, 512], P('fsdp'), may hold values from -0.625 to 0.625
- moment: float32 [512, 14336], P('dp', 'fsdp'), may hold values from -3 to 3
- second: float32 [512, 14336], P('dp', 'fsdp'), may hold values from 0.05 to 1
Outputs:
- moment_new: float32 [512, 14336], P('dp', 'fsdp')
- second_new: float32 [512, 14336], P('dp', 'fsdp')
- dense_update: bfloat16 [8192, 14336], P('fsdp', 'dp')
The draws below stay inside these ranges and needn't reach their ends.
All inputs are finite; a program needn't handle non-finite values.
Results may differ from the reference program's by a relative error of at most 0.019.
Values may be sent and summed in bfloat16 or wider, within the bound.
A program may use at most 64 MiB of HBM per device.

```python
import math
import jax
import jax.numpy as jnp
from jax import lax

D = 8192
FF = 14336
RANK = 512
TOK_DEV = 2048
TOKENS = 32768
N_DP = 16


def level_of(key, dims, cuts, least, high):
    def one(position, parts):
        steps = jax.random.uniform(jax.random.fold_in(jax.random.fold_in(key, 6), position), (parts,), jnp.float32, least / len(cuts), high / len(cuts))
        return jnp.repeat(jnp.exp(steps), dims[position] // parts).reshape((-1,) + (1,) * (len(dims) - position - 1))

    loudness = one(*cuts[0])
    for cut in cuts[1:]:
        loudness = loudness * one(*cut)
    return loudness


def noise(rng, extent, scale, most, pieces=(), kind=jnp.bfloat16):
    values = scale * jax.random.normal(rng, extent, jnp.float32)
    if pieces:
        values = values * level_of(rng, extent, pieces, -0.22, 0.18)
    return jnp.clip(values, -most, most).astype(kind)


def setup_inputs(seed: int = 0) -> dict:
    arg_keys = jax.random.split(jax.random.key(seed), 6)
    acts = noise(arg_keys[0], (D, TOKENS), 1.0, 6.0, ((0, 32), (1, 16)))
    grads = noise(arg_keys[1], (TOKENS, FF), (0.25 * TOKENS ** -0.5), 0.01953125, ((0, 16), (1, 32)))
    basis = noise(arg_keys[2], (D, RANK), (RANK ** -0.5), 0.625, ((0, 32),))
    moment = noise(arg_keys[3], (RANK, FF), 0.5, 3.0, ((0, 16), (1, 32)), jnp.float32)
    second = jnp.clip(jnp.exp(math.log(1.0) - 2.9957323 * jax.random.uniform(arg_keys[4], (RANK, FF), jnp.float32) ** level_of(arg_keys[4], (RANK, FF), ((0, 16), (1, 32)), -0.2, 0.2)), 0.05, 1.0)
    return {"acts": acts, "grads": grads, "basis": basis, "moment": moment, "second": second}


def reference(acts, grads, basis, moment, second):
    projected = lax.dot_general(acts, basis, (((0,), (0,)), ((), ())), preferred_element_type=jnp.float32)
    projected_b = projected.astype(jnp.bfloat16)
    blocks_proj = projected_b.reshape(N_DP, TOK_DEV, RANK)
    blocks_grad = grads.reshape(N_DP, TOK_DEV, FF)

    def add_block(running, operands):
        block_grad = lax.dot_general(operands[0], operands[1], (((0,), (0,)), ((), ())), preferred_element_type=jnp.float32)
        rounded = lax.optimization_barrier(block_grad.astype(jnp.bfloat16))
        return (running + rounded.astype(jnp.float32), None)
    low_grad, unused = lax.scan(add_block, jnp.zeros((RANK, FF), jnp.float32), (blocks_proj, blocks_grad))
    moment_new = 0.9 * moment + 0.1 * low_grad
    second_new = 0.95 * second + 0.05 * low_grad * low_grad
    step_dir = (moment_new / (jnp.sqrt(second_new) + 1e-08)).astype(jnp.bfloat16)
    col_blocks = jnp.transpose(step_dir.reshape(RANK, N_DP, FF // N_DP), (1, 0, 2))

    def project_back(block_step):
        return jnp.dot(basis, block_step, preferred_element_type=jnp.float32).astype(jnp.bfloat16)
    dense_blocks = lax.map(project_back, col_blocks)
    dense_update = jnp.transpose(dense_blocks, (1, 0, 2)).reshape(D, FF)
    return (moment_new, second_new, dense_update)
```

```python
import jax
import jax.numpy as jnp
from jax import lax
from jax.experimental import pallas as pl
from jax.experimental.pallas import tpu as pltpu
from jax.sharding import PartitionSpec as P

F32 = jnp.float32
BF16 = jnp.bfloat16
MESH = pl.DeviceIdType.MESH
TOK = 256
HALF = 256
Q = 128
COLS = 448
ROWS = 32

CORE = 0
RING = 8
XHI = 22
GATH = 24
SHARE = 38
DPX = 54
TRAN = 70
STEP = 72
SHST = 80
COUNT = 89


def kernel(
    acts, basis, grads_hbm, moment, second,
    moment_new, second_new, dense,
    grads, own, csend, crecv, rsend, rrecv, xsend, xrecv, proj, acc, low, lowr, step, steps,
    local_sem, ss, rs,
):
    dp, fs = lax.axis_index("dp"), lax.axis_index("fsdp")
    xl, y = dp // 8, dp % 8
    z, h, c = fs // 4, (fs // 2) % 2, fs % 2

    def at(dz=0, dh=0, dc=0):
        return (dp, ((z + dz + 8) % 8) * 4 + ((h + dh) % 2) * 2 + (c + dc) % 2)

    def dp_at(dx, dy):
        return (((xl + dx) % 2) * 8 + (y + dy) % 8, fs)

    def copy(src, dst, number, device):
        return pltpu.make_async_remote_copy(
            src_ref=src, dst_ref=dst, send_sem=ss.at[number], recv_sem=rs.at[number],
            device_id=device, device_id_type=MESH,
        )

    sent = []

    def start(cp):
        cp.start()
        sent.append(cp)
        return cp

    load = pltpu.make_async_copy(grads_hbm, grads, local_sem.at[0])
    load.start()

    me_diag = dp == z * 2 + h
    barrier = pltpu.get_barrier_semaphore()
    greet = [at(dc=1), at(dh=1), at(1), at(-1), at(2), at(-2)]
    greet += [dp_at(dx, dy) for dx in range(2) for dy in range(8) if (dx, dy) != (0, 0)]
    for device in greet:
        pl.semaphore_signal(barrier, inc=1, device_id=device, device_id_type=MESH)
    for q in range(2):
        @pl.when(jnp.logical_not(jnp.logical_and(me_diag, h == q)))
        def _():
            pl.semaphore_signal(barrier, inc=1, device_id=(z * 2 + q, dp * 2 + c), device_id_type=MESH)

    mine = basis[:, pl.ds(pl.multiple_of(c * HALF, HALF), HALF)].T
    theirs = basis[:, pl.ds(pl.multiple_of((1 - c) * HALF, HALF), HALF)].T
    order = [4, 3, 5, 2, 6, 1, 7, 0]
    cores = {}
    for n, k in enumerate(order):
        tok = pl.ds(pl.multiple_of(((z + k) % 8) * TOK, TOK), TOK)
        chunk = acts[:, tok]
        csend[k] = jnp.dot(theirs, chunk, preferred_element_type=F32).astype(BF16)
        own[k] = jnp.dot(mine, chunk, preferred_element_type=F32)
        if n == 0:
            pl.semaphore_wait(barrier, 23 - jnp.where(me_diag, 1, 0))
        cores[k] = start(copy(csend.at[k], crecv.at[k], CORE + k, at(dc=1)))

    def rows_of(direction, stream):
        half = direction ^ stream
        return slice(half * Q, half * Q + Q)

    def slot(direction, stream, hop):
        return direction * 7 + stream * 4 + hop

    def added(k, rows):
        return own[k, rows, :] + crecv[k, rows, :].astype(F32)

    ring = {}

    def ring_send(direction, stream, hop):
        left = (4 - hop) if stream == 0 else (3 - hop)
        k = (8 - left) % 8 if direction == 0 else left
        n = slot(direction, stream, hop)
        value = added(k, rows_of(direction, stream))
        if hop:
            value = value + rrecv[slot(direction, stream, hop - 1)].astype(F32)
        rsend[n] = value.astype(BF16)
        ring[n] = start(copy(rsend.at[n], rrecv.at[n], RING + n, at(-1 if direction == 0 else 1)))

    cores[4].wait_recv()
    ring_send(0, 0, 0)
    ring_send(1, 0, 0)
    cores[5].wait_recv()
    ring_send(0, 1, 0)
    cores[3].wait_recv()
    ring_send(1, 1, 0)
    for k in order[3:]:
        cores[k].wait_recv()
    for hop in range(1, 4):
        for stream in range(2):
            if stream == 1 and hop == 3:
                continue
            for direction in range(2):
                ring[slot(direction, stream, hop - 1)].wait_recv()
                ring_send(direction, stream, hop)

    pairs = []
    for half in (1, 0):
        rows = slice(half * Q, half * Q + Q)
        total = added(0, rows)
        for direction in range(2):
            stream = direction ^ half
            n = slot(direction, stream, 3 if stream == 0 else 2)
            ring[n].wait_recv()
            total = total + rrecv[n].astype(F32)
        xsend[half] = total.astype(BF16)
        pairs.append(start(copy(xsend.at[half], xrecv.at[half], XHI + half, at(dh=1))))

    def piece(k, half):
        return proj.at[(z + k + 8) % 8, pl.ds(pl.multiple_of(c * HALF + half * Q, Q), Q)]

    gath, shared = {}, {}

    def gath_send(direction, stream, hop):
        half = direction ^ stream
        k = hop if direction == 0 else -hop
        n = slot(direction, stream, hop)
        ref = piece(k, half)
        gath[n] = start(copy(ref, ref, GATH + n, at(-1 if direction == 0 else 1)))

    def share(k, half):
        ref = piece(k, half)
        n = (k % 8) * 2 + half
        shared[n] = start(copy(ref, ref, SHARE + n, at(dc=1)))

    def multiply(k):
        zk = (z + k + 8) % 8
        for half in range(2):
            shared[(k % 8) * 2 + half].wait_recv()
        part = jnp.dot(
            proj[zk], grads[pl.ds(pl.multiple_of(zk * TOK, TOK), TOK), :], preferred_element_type=F32
        )
        if k == 0:
            acc[...] = part
        else:
            acc[...] += part

    for cp, half in zip(pairs, (1, 0)):
        cp.wait_recv()
        total = xsend[half].astype(F32) + xrecv[half].astype(F32)
        proj[z, pl.ds(pl.multiple_of(c * HALF + half * Q, Q), Q), :] = total.astype(BF16)
        gath_send(half, 0, 0)
        gath_send(1 - half, 1, 0)
        share(0, half)
    load.wait()
    multiply(0)
    for hop in range(1, 5):
        for stream in range(2):
            if stream == 1 and hop == 4:
                continue
            for direction in range(2):
                half = direction ^ stream
                gath[slot(direction, stream, hop - 1)].wait_recv()
                if hop < (4 if stream == 0 else 3):
                    gath_send(direction, stream, hop)
                share(hop if direction == 0 else -hop, half)
        if hop > 1:
            multiply(hop - 1)
            multiply(1 - hop)
    multiply(4)

    low[...] = acc[...].astype(BF16)
    dps = []
    for dx, dy in sorted(
        [(dx, dy) for dx in range(2) for dy in range(8) if (dx, dy) != (0, 0)],
        key=lambda o: (-min(o[1], 8 - o[1]), -o[0]),
    ):
        n = dx * 8 + dy
        device = dp_at(dx, dy)
        rows = pl.ds(pl.multiple_of(device[0] * ROWS, ROWS), ROWS)
        dps.append((n, start(copy(low.at[rows], lowr.at[n], DPX + n, device))))
    total = low[pl.ds(pl.multiple_of(dp * ROWS, ROWS), ROWS), :].astype(F32)
    for n, cp in reversed(dps):
        cp.wait_recv()
        total = total + lowr[n].astype(F32)

    m = 0.9 * moment[...] + 0.1 * total
    v = 0.95 * second[...] + 0.05 * total * total
    moment_new[...] = m
    second_new[...] = v
    step[...] = (m / (jnp.sqrt(v) + 1e-8)).astype(BF16)

    def target(q):
        return (z * 2 + q, dp * 2 + c)

    rows = pl.ds(pl.multiple_of(dp * ROWS, ROWS), ROWS)
    group = z * 2 + h
    for q in range(2):
        here = jnp.logical_and(me_diag, h == q)

        @pl.when(here)
        def _():
            steps[c, rows, :] = step[...]

        @pl.when(jnp.logical_not(here))
        def _():
            pltpu.make_async_remote_copy(
                src_ref=step, dst_ref=steps.at[c, rows], send_sem=ss.at[TRAN + q],
                recv_sem=rs.at[TRAN + dp % 2],
                device_id=(group, (dp // 2) * 4 + q * 2 + c), device_id_type=MESH,
            ).start()
    for q in range(2):
        @pl.when(jnp.logical_not(jnp.logical_and(me_diag, h == q)))
        def _():
            pltpu.make_async_remote_copy(
                src_ref=step, dst_ref=steps.at[c, rows], send_sem=ss.at[TRAN + q],
                recv_sem=rs.at[TRAN + q],
                device_id=(group, (dp // 2) * 4 + q * 2 + c), device_id_type=MESH,
            ).wait()

    def srows(k, half=None):
        zk = (z + k + 8) % 8
        if half is None:
            return steps.at[c, pl.ds(pl.multiple_of(zk * 64, 64), 64)]
        return steps.at[c, pl.ds(pl.multiple_of(zk * 64 + half * ROWS, ROWS), ROWS)]

    def pass_on(number, k, dz, half=None):
        ref = srows(k, half)
        return start(copy(ref, ref, STEP + number, at(dz)))

    handed = []

    def hand(number, k, half=None):
        ref = srows(k, half)
        handed.append(start(copy(ref, ref, SHST + number, at(dc=1))))

    far = [pass_on(0, 0, -2), pass_on(1, 0, 2)]
    near = [pass_on(2, 0, -1), pass_on(3, 0, 1)]
    hand(0, 0)
    far[0].wait_recv()
    relay = [pass_on(4, 2, -2, 0), pass_on(6, 2, -1)]
    hand(1, 2)
    far[1].wait_recv()
    relay += [pass_on(5, -2, 2, 1), pass_on(7, -2, 1)]
    hand(2, -2)
    near[0].wait_recv()
    hand(3, 1)
    near[1].wait_recv()
    hand(4, -1)
    relay[1].wait_recv()
    hand(5, 3)
    relay[3].wait_recv()
    hand(6, -3)
    relay[0].wait_recv()
    hand(7, 4, 0)
    relay[2].wait_recv()
    hand(8, -4, 1)
    for cp in handed:
        cp.wait_recv()

    whole = basis[...]
    dense[:, :COLS] = jnp.dot(whole, steps[0], preferred_element_type=F32).astype(BF16)
    dense[:, COLS:] = jnp.dot(whole, steps[1], preferred_element_type=F32).astype(BF16)
    for cp in sent:
        cp.wait_send()


def shards(acts, grads, basis, moment, second):
    vmem = pl.BlockSpec(memory_space=pltpu.VMEM)
    return pl.pallas_call(
        kernel,
        out_shape=(
            jax.ShapeDtypeStruct(moment.shape, F32),
            jax.ShapeDtypeStruct(second.shape, F32),
            jax.ShapeDtypeStruct((256, 896), BF16),
        ),
        in_specs=[vmem, vmem, pl.BlockSpec(memory_space=pl.ANY), vmem, vmem],
        out_specs=(vmem, vmem, vmem),
        scratch_shapes=[
            pltpu.VMEM((2048, COLS), BF16),
            pltpu.VMEM((8, HALF, TOK), F32),
            pltpu.VMEM((8, HALF, TOK), BF16),
            pltpu.VMEM((8, HALF, TOK), BF16),
            pltpu.VMEM((14, Q, TOK), BF16),
            pltpu.VMEM((14, Q, TOK), BF16),
            pltpu.VMEM((2, Q, TOK), BF16),
            pltpu.VMEM((2, Q, TOK), BF16),
            pltpu.VMEM((8, 512, TOK), BF16),
            pltpu.VMEM((512, COLS), F32),
            pltpu.VMEM((512, COLS), BF16),
            pltpu.VMEM((16, ROWS, COLS), BF16),
            pltpu.VMEM((ROWS, COLS), BF16),
            pltpu.VMEM((2, 512, COLS), BF16),
            pltpu.SemaphoreType.DMA((1,)),
            pltpu.SemaphoreType.DMA((COUNT,)),
            pltpu.SemaphoreType.DMA((COUNT,)),
        ],
        compiler_params=pltpu.CompilerParams(
            collective_id=0, has_side_effects=True, vmem_limit_bytes=48 * 2**20
        ),
    )(acts, basis, grads, moment, second)


def solution(mesh):
    in_specs = (P("fsdp", "dp"), P("dp", "fsdp"), P("fsdp", None), P("dp", "fsdp"), P("dp", "fsdp"))
    out_specs = (P("dp", "fsdp"), P("dp", "fsdp"), P("fsdp", "dp"))
    return jax.shard_map(shards, mesh=mesh, in_specs=in_specs, out_specs=out_specs, check_vma=False)
```

```python
import heapq

import jax
import jax.numpy as jnp
from jax import lax
from jax.experimental import pallas as pl
from jax.experimental.pallas import tpu as pltpu
from jax.sharding import PartitionSpec as P

F32 = jnp.float32
BF16 = jnp.bfloat16
MESH = pl.DeviceIdType.MESH
TOK = 256
KEPT = 128
Q = 64
COLS = 448
R = 16
ORDER = (4, 3, 5, 2, 6, 1, 7, 0)

CORE = 0
RING = 2
XHI = 16
GATH = 18
SHARE = 32
DPX = 40
TRAN = 56
STEP = 58
SHST = 66
RELAY = 75
COUNT = 83


class Message:
    def __init__(self, copy, arrival):
        self.copy, self.arrival = copy, arrival


class Plan:
    def __init__(self):
        self.now, self.heap, self.count, self.free = 0.0, [], 0, {}
        self.sent = []

    def spend(self, cost):
        self.now += cost

    def arrive(self, copy, path, kib):
        message = Message(copy, self.arrival(path, kib))
        self.sent.append(message)
        return message

    def arrival(self, path, kib):
        if path is None:
            return self.now + 0.85 + kib / 1000
        each = kib * 0.0227
        start = max([self.now] + [self.free.get(link, 0.0) for link, _ in path])
        for link, hops in path:
            self.free[link] = max(self.free.get(link, 0.0), self.now) + each * hops
        self.spend(0.03)
        return start + each + 1.95 + 0.6 * sum(hops for _, hops in path)

    def when(self, messages, action, ready=0.0):
        ready = max([ready] + [m.arrival for m in messages])
        heapq.heappush(self.heap, (ready, self.count, messages, action))
        self.count += 1

    def run(self):
        while self.heap:
            ready, _, messages, action = heapq.heappop(self.heap)
            while self.sent and self.sent[0].arrival < self.now - 1 and self.now + 0.2 < ready:
                self.sent.pop(0).copy.wait_send()
                self.spend(0.05)
            self.now = max(self.now, ready)
            for m in messages:
                m.copy.wait_recv()
            action()


def kernel(
    acts_hbm, basis_hbm, grads_hbm, moment_hbm, second_hbm,
    moment_new, second_new, dense,
    acts, basis, grads, moment, second,
    lhs, feats, own, csend, crecv, rsend, rrecv, xsend, xrecv, psend, precv, pown, fsend, frecv, proj, acc, low, lowr, step, steps, wide,
    local_sem, ss, rs,
):
    dp, fs = lax.axis_index("dp"), lax.axis_index("fsdp")
    xl, y = dp // 8, dp % 8
    z, h, c = fs // 4, (fs // 2) % 2, fs % 2

    def at(dz=0, dh=0, dc=0):
        return (dp, ((z + dz + 8) % 8) * 4 + ((h + dh) % 2) * 2 + (c + dc) % 2)

    def dp_at(dx, dy):
        return (((xl + dx) % 2) * 8 + (y + dy) % 8, fs)

    plan = Plan()

    def send(s, src, dst, number, device, path, kib):
        cp = pltpu.make_async_remote_copy(
            src_ref=src, dst_ref=dst, send_sem=ss.at[s * COUNT + number], recv_sem=rs.at[s * COUNT + number],
            device_id=device, device_id_type=MESH,
        )
        cp.start()
        return plan.arrive(cp, path, kib)

    diagonal = jnp.logical_and(dp == z * 2 + h, y == z)
    barrier = pltpu.get_barrier_semaphore()
    greet = [at(dc=1), at(dh=1), at(1), at(-1), at(2), at(-2)]
    greet += [dp_at(dx, dy) for dx in range(2) for dy in range(8) if (dx, dy) != (0, 0)]
    for device in greet:
        pl.semaphore_signal(barrier, inc=1, device_id=device, device_id_type=MESH)
    loads = []
    for n, (src, dst) in enumerate((
        (basis_hbm, basis), (acts_hbm, acts), (grads_hbm, grads), (moment_hbm, moment), (second_hbm, second),
    )):
        loads.append(pltpu.make_async_copy(src, dst, local_sem.at[n]))
        loads[-1].start()

    loads[0].wait()
    for j in range(4):
        block = basis[:, j * 128 : j * 128 + 128].T
        place = jnp.where(c == j // 2, 1, 0)
        for b in range(4):
            for s in range(2):
                row = ((j % 2) * 4 + b) * R
                lhs[s, place, row : row + R] = block[b * 32 + s * R : b * 32 + s * R + R]
    loads[1].wait()

    def rows_of(half):
        return slice(half * Q, half * Q + Q)

    def slot(direction, half, hop):
        return direction * 7 + (0 if hop == 0 else 1 + (hop - 1) * 2 + half)

    def zlink(direction):
        return "z-" if direction == 0 else "z+"

    def partial(s, n):
        k = ORDER[n]
        tok = pl.ds(pl.multiple_of(((z + k) % 8) * TOK, TOK), TOK)
        both = jnp.dot(lhs[s].reshape(2 * KEPT, 256), acts[:, tok], preferred_element_type=F32)
        csend[s, n] = both[:KEPT].astype(BF16)
        own[s, n] = both[KEPT:]
        plan.spend(0.15)

    def exchange(s, part):
        first, last = ((0, 3), (3, 8))[part]
        for n in range(first, last):
            partial(s, n)
        if s == 1 and part == 0:
            pl.semaphore_wait(barrier, 21)
        place = pl.ds(first, last - first)
        m = send(s, csend.at[s, place], crecv.at[s, place], CORE + part, at(dc=1), None, 64 * (last - first))
        plan.when([m], lambda: ((pair_first, pair_rest), (reduce_start, reduce_rest))[s][part](s))

    def added(s, k, half):
        n = ORDER.index(k % 8)
        return own[s, n, rows_of(half), :] + crecv[s, n, rows_of(half), :].astype(F32)

    waiting = {}

    def ring_send(s, direction, half, hop, value):
        n = slot(direction, half, hop)
        rsend[s, n] = value.astype(BF16)
        plan.spend(0.08)
        hops = 2 if hop == 0 else 1
        sign = -1 if direction == 0 else 1
        m = send(s, rsend.at[s, n], rrecv.at[s, n], RING + n, at(sign * hops), [(zlink(direction), hops)], 32)
        if hop == 0:
            waiting[s, direction, half] = m
        else:
            plan.when([m], lambda: ring_next(s, direction, half, hop))

    def reduce_start(s):
        for direction in range(2):
            ring_send(s, direction, direction, 0, added(s, 4, direction))
        for half in range(2):
            for direction in range(2):
                k = 5 if direction == 0 else 3
                ring_send(s, direction, half ^ direction ^ 1, 1, added(s, k, half ^ direction ^ 1))

    ready = {0: False, 1: False}
    held = {0: [], 1: []}

    def reduce_rest(s):
        ready[s] = True
        for action in held[s]:
            action()

    sums = {}

    def ring_next(s, direction, half, hop):
        if not ready[s]:
            held[s].append(lambda: ring_next(s, direction, half, hop))
            return
        arrived = rrecv[s, slot(direction, half, hop)].astype(F32)
        if hop == 1 and half == direction:
            m = waiting[s, direction, half]
            m.copy.wait_recv()
            plan.now = max(plan.now, m.arrival)
            arrived = arrived + rrecv[s, slot(direction, half, 0)].astype(F32)
        if hop < 3:
            k = hop - 3 if direction == 0 else 3 - hop
            ring_send(s, direction, half, hop + 1, added(s, k, half) + arrived)
            return
        sums.setdefault((s, half), []).append(direction)
        if len(sums[s, half]) == 2:
            total = added(s, 0, half)
            for d in range(2):
                total = total + rrecv[s, slot(d, half, 3)].astype(F32)
            xsend[s, half] = total.astype(BF16)
            plan.spend(0.1)
            m = send(s, xsend.at[s, half], xrecv.at[s, half], XHI + half, at(dh=1), [("x", 1), ("x2", 1)], 32)
            plan.when([m], lambda: gather_start(s, half))

    mine = pl.multiple_of(h * Q, Q)
    theirs = pl.multiple_of((1 - h) * Q, Q)

    def pair(s, part):
        first, last = ((0, 3), (3, 8))[part]
        for n in range(first, last):
            for rows, out in ((theirs, None), (mine, own)):
                rows = pl.ds(rows, Q)
                value = own[s, n, rows, :] + crecv[s, n, rows, :].astype(F32)
                if out is None:
                    psend[n] = value.astype(BF16)
                else:
                    pown[n] = value
            plan.spend(0.1)
        place = pl.ds(first, last - first)
        m = send(
            s, psend.at[place], precv.at[place], XHI + part, at(dh=1), [("x", 1), ("x2", 1)], 32 * (last - first)
        )
        plan.when([m], lambda: (paired_first, paired_rest)[part](s))

    def pair_first(s):
        pair(s, 0)

    def pair_rest(s):
        pair(s, 1)

    def paired(k):
        n = ORDER.index(k % 8)
        return pown[n] + precv[n].astype(F32)

    def pair_send(s, n, direction, hops, value, action):
        rows = slice(0, value.shape[0])
        fsend[n, rows, :] = value.astype(BF16)
        plan.spend(0.05)
        sign = -1 if direction == 0 else 1
        m = send(
            s, fsend.at[n, rows], frecv.at[n, rows], RING + n, at(sign * hops), [(zlink(direction), hops)],
            value.shape[0] // 2,
        )
        plan.when([m], action)

    need = {}

    def counted(key, limit, action):
        need[key] = need.get(key, 0) + 1
        if need[key] == limit:
            action()

    def paired_first(s):
        for direction in range(2):
            value = paired(4)[direction * 32 : direction * 32 + 32]
            pair_send(s, direction * 4, direction, 2, value, lambda d=direction: pair_collect(s, d))
        for direction in range(2):
            value = paired(-3 if direction == 0 else 3)
            pair_send(s, direction * 4 + 1, direction, 1, value, lambda d=direction: pair_collect(s, d))

    def paired_rest(s):
        for direction in range(2):
            value = paired(-1 if direction == 0 else 1)
            pair_send(s, direction * 4 + 2, direction, 1, value, lambda: pair_total(s))
        for direction in range(2):
            pair_collect(s, direction)

    def pair_collect(s, direction):
        def collected():
            n = direction * 4
            value = paired(-2 if direction == 0 else 2) + frecv[n + 1].astype(F32)
            half = frecv[n, 0:32, :].astype(F32)
            zero = jnp.zeros_like(half)
            value = value + jnp.concatenate([half, zero] if direction == 0 else [zero, half], axis=0)
            pair_send(s, n + 3, direction, 2, value, lambda: pair_total(s))

        counted(("collect", direction), 3, collected)

    def pair_total(s):
        def totalled():
            value = paired(0)
            for n in (2, 3, 6, 7):
                value = value + frecv[n].astype(F32)
            proj[s, z, pl.ds(pl.multiple_of(c * KEPT + h * Q, Q), Q), :] = value.astype(BF16)
            plan.spend(0.1)
            pair_gather(s)

        counted("total", 4, totalled)

    def fpiece(s, k, half=None):
        row = c * KEPT + h * Q + (0 if half is None else half * 32)
        rows = pl.ds(pl.multiple_of(row, 32), Q if half is None else 32)
        return proj.at[s, (z + k + 8) % 8, rows]

    def pair_gather(s):
        def relay(k):
            ref = fpiece(s, k)
            m = send(s, ref, ref, RELAY + k % 8, at(dh=1), [("x", 1), ("x2", 1)], 32)
            plan.when([m], lambda: arrived_piece(s, k))
            arrived_piece(s, k)

        def pass_on(number, k, dz, action, half=None):
            ref = fpiece(s, k, half)
            link = zlink(0 if dz < 0 else 1)
            m = send(s, ref, ref, GATH + number, at(dz), [(link, abs(dz))], 32 if half is None else 16)
            plan.when([m], action)

        def farthest():
            counted("farthest", 2, lambda: relay(4))

        def from_above():
            pass_on(4, 2, -2, farthest, 0)
            pass_on(6, 2, -1, lambda: relay(3))
            relay(2)

        def from_below():
            pass_on(5, -2, 2, farthest, 1)
            pass_on(7, -2, 1, lambda: relay(-3))
            relay(-2)

        pass_on(0, 0, -2, from_above)
        pass_on(1, 0, 2, from_below)
        pass_on(2, 0, -1, lambda: relay(1))
        pass_on(3, 0, 1, lambda: relay(-1))
        relay(0)

    def piece(s, k, half):
        return proj.at[s, (z + k + 8) % 8, pl.ds(pl.multiple_of(c * KEPT + half * Q, Q), Q)]

    def gath_send(s, direction, half, hop, k, hops=1):
        sign = -1 if direction == 0 else 1
        ref = piece(s, k, half)
        n = slot(direction, half, 3 - hop) if hops == 1 else slot(direction, half, 0)
        m = send(s, ref, ref, GATH + n, at(sign * hops), [(zlink(direction), hops)], 32)
        plan.when([m], lambda: gathered(s, direction, half, hop + hops))

    have = {}

    def arrived_piece(s, k):
        have[s, k] = have.get((s, k), 0) + 1
        if have[s, k] == 2:
            ref = proj.at[s, (z + k + 8) % 8, pl.ds(pl.multiple_of(c * KEPT, KEPT), KEPT)]
            m = send(s, ref, ref, SHARE + k % 8, at(dc=1), None, 64)
            plan.when([m], lambda: multiply(s, k))

    def gather_start(s, half):
        total = xsend[s, half].astype(F32) + xrecv[s, half].astype(F32)
        proj[s, z, pl.ds(pl.multiple_of(c * KEPT + half * Q, Q), Q), :] = total.astype(BF16)
        plan.spend(0.1)
        for direction in range(2):
            gath_send(s, direction, half, 0, 0)
        arrived_piece(s, 0)

    def gathered(s, direction, half, hop):
        sign = 1 if direction == 0 else -1
        if hop == 2 and half == direction:
            gath_send(s, direction, half, 2, sign * 2, hops=2)
        if hop < 3:
            gath_send(s, direction, half, hop, sign * hop)
        arrived_piece(s, sign * hop if hop < 4 else 4)

    loaded = []
    done = {0: 0, 1: 0}

    def multiply(s, k):
        if not loaded:
            loads[2].wait()
            loaded.append(True)
        zk = (z + k + 8) % 8
        part = lax.dot_general(
            proj[s, zk], grads[:, pl.ds(pl.multiple_of(zk * TOK, TOK), TOK)],
            (((1,), (1,)), ((), ())), preferred_element_type=F32,
        )
        plan.spend(0.3)
        done[s] += 1
        if done[s] == 1:
            acc[s] = part
        elif done[s] < 8:
            acc[s] += part
        else:
            low[s] = (acc[s] + part).astype(BF16)
            over_dp(s)

    def over_dp(s):
        messages = []
        offsets = [(dx, dy) for dx in range(2) for dy in range(8) if (dx, dy) != (0, 0)]
        for dx, dy in sorted(offsets, key=lambda o: (-min(o[1], 8 - o[1]), -o[0])):
            n = dx * 8 + dy
            device = dp_at(dx, dy)
            path = [("y+", dy)] if dy < 4 else [("y-", 8 - dy)] if dy > 4 else [("y+", 2), ("y-", 2)]
            rows = pl.ds(pl.multiple_of(device[0] * R, R), R)
            messages.append((n, send(s, low.at[s, rows], lowr.at[s, n], DPX + n, device, path, 16)))
        plan.when([m for _, m in messages], lambda: adam(s, [n for n, _ in messages]))

    def adam(s, numbers):
        if "adam" not in need:
            need["adam"] = 1
            loads[3].wait()
            loads[4].wait()
        total = low[s, pl.ds(pl.multiple_of(dp * R, R), R), :].astype(F32)
        for n in numbers:
            total = total + lowr[s, n].astype(F32)
        rows = slice(s * R, s * R + R)
        m = 0.9 * moment[rows] + 0.1 * total
        v = 0.95 * second[rows] + 0.05 * total * total
        moment_new[rows] = m
        second_new[rows] = v
        step[s] = (m / (jnp.sqrt(v) + 1e-8)).astype(BF16)
        plan.spend(0.3)

        place = pl.ds(pl.multiple_of(y * R, R), R)
        for q in range(2):
            here = jnp.logical_and(diagonal, h == q)

            @pl.when(here)
            def _():
                steps[c, s, xl, place, :] = step[s]

            @pl.when(jnp.logical_not(here))
            def _():
                turn(s, q, xl).start()
        plan.when([], lambda: turned(s), ready=plan.now + 6)

    def turn(s, q, origin):
        place = pl.ds(pl.multiple_of(y * R, R), R)
        return pltpu.make_async_remote_copy(
            src_ref=step.at[s], dst_ref=steps.at[c, s, xl, place], send_sem=ss.at[s * COUNT + TRAN + q],
            recv_sem=rs.at[s * COUNT + TRAN + origin],
            device_id=(z * 2 + h, y * 4 + q * 2 + c), device_id_type=MESH,
        )

    def turned(s):
        for q in range(2):
            @pl.when(jnp.logical_not(jnp.logical_and(diagonal, xl == q)))
            def _():
                turn(s, q, q).wait_recv()
        spread(s)

    def srows(s, k, half=None):
        place = pl.ds(pl.multiple_of(((z + k + 8) % 8) * R, R), R)
        if half is None:
            return steps.at[c, s, :, place]
        return steps.at[c, s, half, place]

    def spread(s):
        def hand(number, k, half=None):
            ref = srows(s, k, half)
            m = send(s, ref, ref, SHST + number, at(dc=1), None, 32)
            plan.when([m], lambda: counted(("other", s), 9, lambda: finished(s, "other")))
            if number:
                counted(("this", s), 8, lambda: finished(s, "this"))

        def pass_on(number, k, dz, action, half=None):
            ref = srows(s, k, half)
            link = zlink(0 if dz < 0 else 1)
            m = send(s, ref, ref, STEP + number, at(dz), [(link, abs(dz))], 32 if half is None else 16)
            plan.when([m], action)

        def from_above():
            pass_on(4, 2, -2, lambda: hand(7, 4, 0), 0)
            pass_on(6, 2, -1, lambda: hand(5, 3))
            hand(1, 2)

        def from_below():
            pass_on(5, -2, 2, lambda: hand(8, 4, 1), 1)
            pass_on(7, -2, 1, lambda: hand(6, -3))
            hand(2, -2)

        pass_on(0, 0, -2, from_above)
        pass_on(1, 0, 2, from_below)
        pass_on(2, 0, -1, lambda: hand(3, 1))
        pass_on(3, 0, 1, lambda: hand(4, -1))
        hand(0, 0)

    def natural():
        for s in range(2):
            both = [lhs[s, jnp.where(c == core, 1, 0)] for core in range(2)]
            feats[s] = jnp.concatenate(both, axis=0).T

    ends = []

    def finished(s, which):
        columns = c if which == "this" else 1 - c
        value = jnp.dot(feats[s], steps[columns, s].reshape(256, COLS), preferred_element_type=F32)
        if which not in ends:
            wide[columns] = value
        else:
            wide[columns] += value
        plan.spend(0.2)
        ends.append(which)
        if len(ends) == 4:
            for half in range(2):
                dense[:, half * COLS : half * COLS + COLS] = wide[half].astype(BF16)

    exchange(1, 0)
    plan.when([], lambda: exchange(0, 0), ready=plan.now)
    plan.when([], lambda: exchange(1, 1), ready=plan.now + 0.01)
    plan.when([], lambda: exchange(0, 1), ready=plan.now + 0.02)
    plan.when([], natural, ready=plan.now + 5)
    plan.run()
    for m in plan.sent:
        m.copy.wait_send()
    for s in range(2):
        for q in range(2):
            @pl.when(jnp.logical_not(jnp.logical_and(diagonal, h == q)))
            def _():
                turn(s, q, 0).wait_send()


def store(a, b, c, a_out, b_out, c_out):
    a_out[...] = a[...]
    b_out[...] = b[...]
    c_out[...] = c[...]


def shards(acts, grads, basis, moment, second):
    vmem = pl.BlockSpec(memory_space=pltpu.VMEM)
    hbm = pl.BlockSpec(memory_space=pltpu.HBM)
    results = pl.pallas_call(
        kernel,
        out_shape=(
            jax.ShapeDtypeStruct(moment.shape, F32),
            jax.ShapeDtypeStruct(second.shape, F32),
            jax.ShapeDtypeStruct((256, 896), BF16),
        ),
        in_specs=[hbm] * 5,
        out_specs=(vmem, vmem, vmem),
        scratch_shapes=[
            pltpu.VMEM((256, 2048), BF16),
            pltpu.VMEM((256, 512), BF16),
            pltpu.VMEM((COLS, 2048), BF16),
            pltpu.VMEM((32, COLS), F32),
            pltpu.VMEM((32, COLS), F32),
            pltpu.VMEM((2, 2, KEPT, 256), BF16),
            pltpu.VMEM((2, 256, 256), BF16),
            pltpu.VMEM((2, 8, KEPT, TOK), F32),
            pltpu.VMEM((2, 8, KEPT, TOK), BF16),
            pltpu.VMEM((2, 8, KEPT, TOK), BF16),
            pltpu.VMEM((2, 14, Q, TOK), BF16),
            pltpu.VMEM((2, 14, Q, TOK), BF16),
            pltpu.VMEM((2, 2, Q, TOK), BF16),
            pltpu.VMEM((2, 2, Q, TOK), BF16),
            pltpu.VMEM((8, Q, TOK), BF16),
            pltpu.VMEM((8, Q, TOK), BF16),
            pltpu.VMEM((8, Q, TOK), F32),
            pltpu.VMEM((8, Q, TOK), BF16),
            pltpu.VMEM((8, Q, TOK), BF16),
            pltpu.VMEM((2, 8, 2 * KEPT, TOK), BF16),
            pltpu.VMEM((2, 2 * KEPT, COLS), F32),
            pltpu.VMEM((2, 2 * KEPT, COLS), BF16),
            pltpu.VMEM((2, 16, R, COLS), BF16),
            pltpu.VMEM((2, R, COLS), BF16),
            pltpu.VMEM((2, 2, 2, 128, COLS), BF16),
            pltpu.VMEM((2, 256, COLS), F32),
            pltpu.SemaphoreType.DMA((5,)),
            pltpu.SemaphoreType.DMA((2 * COUNT,)),
            pltpu.SemaphoreType.DMA((2 * COUNT,)),
        ],
        compiler_params=pltpu.CompilerParams(
            collective_id=0, has_side_effects=True, vmem_limit_bytes=60 * 2**20
        ),
    )(acts, basis, grads.T, moment, second)
    return pl.pallas_call(
        store,
        out_shape=tuple(jax.ShapeDtypeStruct(r.shape, r.dtype) for r in results),
        in_specs=[vmem] * 3,
        out_specs=(vmem,) * 3,
    )(*results)


def solution(mesh):
    in_specs = (P("fsdp", "dp"), P("dp", "fsdp"), P("fsdp", None), P("dp", "fsdp"), P("dp", "fsdp"))
    out_specs = (P("dp", "fsdp"), P("dp", "fsdp"), P("fsdp", "dp"))
    return jax.shard_map(shards, mesh=mesh, in_specs=in_specs, out_specs=out_specs, check_vma=False)
```

```python
import heapq

import jax
import jax.numpy as jnp
from jax import lax
from jax.experimental import pallas as pl
from jax.experimental.pallas import tpu as pltpu
from jax.sharding import PartitionSpec as P

F32 = jnp.float32
BF16 = jnp.bfloat16
MESH = pl.DeviceIdType.MESH
TOK = 256
KEPT = 128
Q = 64
COLS = 448
WIDE = 512
R = 16
DP_PAIR = (True, True)
ORDER = (4, 3, 5, 2, 6, 1, 7, 0)

CORE = 0
RING = 2
XHI = 16
GATH = 18
SHARE = 32
DPX = 40
TRAN = 56
STEP = 58
SHST = 66
RELAY = 75
COUNT = 83


class Message:
    def __init__(self, copy, arrival):
        self.copy, self.arrival = copy, arrival


class Plan:
    def __init__(self):
        self.now, self.heap, self.count, self.free = 0.0, [], 0, {}
        self.sent = []

    def spend(self, cost):
        self.now += cost

    def arrive(self, copy, path, kib):
        message = Message(copy, self.arrival(path, kib))
        self.sent.append(message)
        return message

    def arrival(self, path, kib):
        if path is None:
            return self.now + 0.85 + kib / 1000
        each = kib * 0.0227
        start = max([self.now] + [self.free.get(link, 0.0) for link, _ in path])
        for link, hops in path:
            self.free[link] = max(self.free.get(link, 0.0), self.now) + each * hops
        self.spend(0.03)
        return start + each + 1.95 + 0.6 * sum(hops for _, hops in path)

    def when(self, messages, action, ready=0.0):
        ready = max([ready] + [m.arrival for m in messages])
        heapq.heappush(self.heap, (ready, self.count, messages, action))
        self.count += 1

    def run(self):
        while self.heap:
            ready, _, messages, action = heapq.heappop(self.heap)
            while self.sent and self.sent[0].arrival < self.now - 1 and self.now + 0.2 < ready:
                self.sent.pop(0).copy.wait_send()
                self.spend(0.05)
            self.now = max(self.now, ready)
            for m in messages:
                m.copy.wait_recv()
            action()


def kernel(
    acts_hbm, basis_hbm, grads_hbm, moment_hbm, second_hbm,
    moment_new, second_new, dense,
    acts, basis, grads, moment, second,
    lhs, feats, own, csend, crecv, rsend, rrecv, xsend, xrecv, psend, precv, pown, fsend, frecv, proj, acc, low, lowr, lowx, step, steps, wide,
    local_sem, ss, rs,
):
    dp, fs = lax.axis_index("dp"), lax.axis_index("fsdp")
    xl, y = dp // 8, dp % 8
    z, h, c = fs // 4, (fs // 2) % 2, fs % 2

    def at(dz=0, dh=0, dc=0):
        return (dp, ((z + dz + 8) % 8) * 4 + ((h + dh) % 2) * 2 + (c + dc) % 2)

    def dp_at(dx, dy):
        return (((xl + dx) % 2) * 8 + (y + dy) % 8, fs)

    plan = Plan()

    def send(s, src, dst, number, device, path, kib):
        cp = pltpu.make_async_remote_copy(
            src_ref=src, dst_ref=dst, send_sem=ss.at[s * COUNT + number], recv_sem=rs.at[s * COUNT + number],
            device_id=device, device_id_type=MESH,
        )
        cp.start()
        return plan.arrive(cp, path, kib)

    loads = []
    for n, (src, dst) in enumerate((
        (basis_hbm, basis), (acts_hbm, acts), (grads_hbm, grads), (moment_hbm, moment), (second_hbm, second),
    )):
        loads.append(pltpu.make_async_copy(src, dst, local_sem.at[n]))
    loads[0].start()
    loads[1].start()

    barrier = pltpu.get_barrier_semaphore()
    greet = [at(dc=1), at(dh=1), at(1), at(-1), at(2), at(-2)]
    greet += [dp_at(1, 0)] + [dp_at(0, dy) for dy in range(1, 8)]
    for device in greet:
        pl.semaphore_signal(barrier, inc=1, device_id=device, device_id_type=MESH)
    loads[0].wait()
    for j in range(4):
        block = basis[:, j * 128 : j * 128 + 128].T
        place = jnp.where(c == j // 2, 1, 0)
        for b in range(4):
            for s in range(2):
                row = ((j % 2) * 4 + b) * R
                lhs[s, place, row : row + R] = block[b * 32 + s * R : b * 32 + s * R + R]
    loads[1].wait()

    def rows_of(half):
        return slice(half * Q, half * Q + Q)

    def slot(direction, half, hop):
        return direction * 7 + (0 if hop == 0 else 1 + (hop - 1) * 2 + half)

    def zlink(direction):
        return "z-" if direction == 0 else "z+"

    def partial(s, n):
        k = ORDER[n]
        tok = pl.ds(pl.multiple_of(((z + k) % 8) * TOK, TOK), TOK)
        both = jnp.dot(lhs[s].reshape(2 * KEPT, 256), acts[:, tok], preferred_element_type=F32)
        csend[s, n] = both[:KEPT].astype(BF16)
        own[s, n] = both[KEPT:]
        plan.spend(0.15)

    def exchange(s, part):
        first, last = ((0, 3), (3, 8))[part]
        for n in range(first, last):
            partial(s, n)
        if s == 1 and part == 0:
            pl.semaphore_wait(barrier, 14)
        place = pl.ds(first, last - first)
        m = send(s, csend.at[s, place], crecv.at[s, place], CORE + part, at(dc=1), None, 64 * (last - first))
        plan.when([m], lambda: ((pair_first, pair_rest), (reduce_start, reduce_rest))[s][part](s))

    def added(s, k, half):
        n = ORDER.index(k % 8)
        return own[s, n, rows_of(half), :] + crecv[s, n, rows_of(half), :].astype(F32)

    waiting = {}

    def ring_send(s, direction, half, hop, value):
        n = slot(direction, half, hop)
        rsend[s, n] = value.astype(BF16)
        plan.spend(0.08)
        hops = 2 if hop == 0 else 1
        sign = -1 if direction == 0 else 1
        m = send(s, rsend.at[s, n], rrecv.at[s, n], RING + n, at(sign * hops), [(zlink(direction), hops)], 32)
        if hop == 0:
            waiting[s, direction, half] = m
        else:
            plan.when([m], lambda: ring_next(s, direction, half, hop))

    def reduce_start(s):
        for direction in range(2):
            ring_send(s, direction, direction, 0, added(s, 4, direction))
        for half in range(2):
            for direction in range(2):
                k = 5 if direction == 0 else 3
                ring_send(s, direction, half ^ direction ^ 1, 1, added(s, k, half ^ direction ^ 1))

    ready = {0: False, 1: False}
    held = {0: [], 1: []}

    def reduce_rest(s):
        ready[s] = True
        for action in held[s]:
            action()

    sums = {}

    def ring_next(s, direction, half, hop):
        if not ready[s]:
            held[s].append(lambda: ring_next(s, direction, half, hop))
            return
        arrived = rrecv[s, slot(direction, half, hop)].astype(F32)
        if hop == 1 and half == direction:
            m = waiting[s, direction, half]
            m.copy.wait_recv()
            plan.now = max(plan.now, m.arrival)
            arrived = arrived + rrecv[s, slot(direction, half, 0)].astype(F32)
        if hop < 3:
            k = hop - 3 if direction == 0 else 3 - hop
            ring_send(s, direction, half, hop + 1, added(s, k, half) + arrived)
            return
        sums.setdefault((s, half), []).append(direction)
        if len(sums[s, half]) == 2:
            total = added(s, 0, half)
            for d in range(2):
                total = total + rrecv[s, slot(d, half, 3)].astype(F32)
            xsend[s, half] = total.astype(BF16)
            plan.spend(0.1)
            m = send(s, xsend.at[s, half], xrecv.at[s, half], XHI + half, at(dh=1), [("x", 1), ("x2", 1)], 32)
            plan.when([m], lambda: gather_start(s, half))

    mine = pl.multiple_of(h * Q, Q)
    theirs = pl.multiple_of((1 - h) * Q, Q)

    def pair(s, part):
        first, last = ((0, 3), (3, 8))[part]
        for n in range(first, last):
            for rows, out in ((theirs, None), (mine, own)):
                rows = pl.ds(rows, Q)
                value = own[s, n, rows, :] + crecv[s, n, rows, :].astype(F32)
                if out is None:
                    psend[n] = value.astype(BF16)
                else:
                    pown[n] = value
            plan.spend(0.1)
        place = pl.ds(first, last - first)
        m = send(
            s, psend.at[place], precv.at[place], XHI + part, at(dh=1), [("x", 1), ("x2", 1)], 32 * (last - first)
        )
        plan.when([m], lambda: (paired_first, paired_rest)[part](s))

    def pair_first(s):
        pair(s, 0)

    def pair_rest(s):
        pair(s, 1)

    def paired(k):
        n = ORDER.index(k % 8)
        return pown[n] + precv[n].astype(F32)

    def pair_send(s, n, direction, hops, value, action):
        rows = slice(0, value.shape[0])
        fsend[n, rows, :] = value.astype(BF16)
        plan.spend(0.05)
        sign = -1 if direction == 0 else 1
        m = send(
            s, fsend.at[n, rows], frecv.at[n, rows], RING + n, at(sign * hops), [(zlink(direction), hops)],
            value.shape[0] // 2,
        )
        plan.when([m], action)

    need = {}

    def counted(key, limit, action):
        need[key] = need.get(key, 0) + 1
        if need[key] == limit:
            action()

    def paired_first(s):
        for direction in range(2):
            value = paired(4)[direction * 32 : direction * 32 + 32]
            pair_send(s, direction * 4, direction, 2, value, lambda d=direction: pair_collect(s, d))
        for direction in range(2):
            value = paired(-3 if direction == 0 else 3)
            pair_send(s, direction * 4 + 1, direction, 1, value, lambda d=direction: pair_collect(s, d))

    def paired_rest(s):
        for direction in range(2):
            value = paired(-1 if direction == 0 else 1)
            pair_send(s, direction * 4 + 2, direction, 1, value, lambda: pair_total(s))
        for direction in range(2):
            pair_collect(s, direction)

    def pair_collect(s, direction):
        def collected():
            n = direction * 4
            value = paired(-2 if direction == 0 else 2) + frecv[n + 1].astype(F32)
            half = frecv[n, 0:32, :].astype(F32)
            zero = jnp.zeros_like(half)
            value = value + jnp.concatenate([half, zero] if direction == 0 else [zero, half], axis=0)
            pair_send(s, n + 3, direction, 2, value, lambda: pair_total(s))

        counted(("collect", direction), 3, collected)

    def pair_total(s):
        def totalled():
            value = paired(0)
            for n in (2, 3, 6, 7):
                value = value + frecv[n].astype(F32)
            proj[s, z, pl.ds(pl.multiple_of(c * KEPT + h * Q, Q), Q), :] = value.astype(BF16)
            plan.spend(0.1)
            pair_gather(s)

        counted("total", 4, totalled)

    def fpiece(s, k, half=None):
        row = c * KEPT + h * Q + (0 if half is None else half * 32)
        rows = pl.ds(pl.multiple_of(row, 32), Q if half is None else 32)
        return proj.at[s, (z + k + 8) % 8, rows]

    def pair_gather(s):
        def relay(k):
            ref = fpiece(s, k)
            m = send(s, ref, ref, RELAY + k % 8, at(dh=1), [("x", 1), ("x2", 1)], 32)
            plan.when([m], lambda: arrived_piece(s, k))
            arrived_piece(s, k)

        def pass_on(number, k, dz, action, half=None):
            ref = fpiece(s, k, half)
            link = zlink(0 if dz < 0 else 1)
            m = send(s, ref, ref, GATH + number, at(dz), [(link, abs(dz))], 32 if half is None else 16)
            plan.when([m], action)

        def farthest():
            counted("farthest", 2, lambda: relay(4))

        def from_above():
            pass_on(4, 2, -2, farthest, 0)
            pass_on(6, 2, -1, lambda: relay(3))
            relay(2)

        def from_below():
            pass_on(5, -2, 2, farthest, 1)
            pass_on(7, -2, 1, lambda: relay(-3))
            relay(-2)

        pass_on(0, 0, -2, from_above)
        pass_on(1, 0, 2, from_below)
        pass_on(2, 0, -1, lambda: relay(1))
        pass_on(3, 0, 1, lambda: relay(-1))
        relay(0)

    def piece(s, k, half):
        return proj.at[s, (z + k + 8) % 8, pl.ds(pl.multiple_of(c * KEPT + half * Q, Q), Q)]

    def gath_send(s, direction, half, hop, k, hops=1):
        sign = -1 if direction == 0 else 1
        ref = piece(s, k, half)
        n = slot(direction, half, 3 - hop) if hops == 1 else slot(direction, half, 0)
        m = send(s, ref, ref, GATH + n, at(sign * hops), [(zlink(direction), hops)], 32)
        plan.when([m], lambda: gathered(s, direction, half, hop + hops))

    have = {}

    def arrived_piece(s, k):
        have[s, k] = have.get((s, k), 0) + 1
        if have[s, k] == 2:
            ref = proj.at[s, (z + k + 8) % 8, pl.ds(pl.multiple_of(c * KEPT, KEPT), KEPT)]
            m = send(s, ref, ref, SHARE + k % 8, at(dc=1), None, 64)
            plan.when([m], lambda: multiply(s, k))

    def gather_start(s, half):
        total = xsend[s, half].astype(F32) + xrecv[s, half].astype(F32)
        proj[s, z, pl.ds(pl.multiple_of(c * KEPT + half * Q, Q), Q), :] = total.astype(BF16)
        plan.spend(0.1)
        for direction in range(2):
            gath_send(s, direction, half, 0, 0)
        arrived_piece(s, 0)

    def gathered(s, direction, half, hop):
        sign = 1 if direction == 0 else -1
        if hop == 2 and half == direction:
            gath_send(s, direction, half, 2, sign * 2, hops=2)
        if hop < 3:
            gath_send(s, direction, half, hop, sign * hop)
        arrived_piece(s, sign * hop if hop < 4 else 4)

    loaded = []
    done = {0: 0, 1: 0}

    def multiply(s, k):
        if not loaded:
            loads[2].wait()
            loaded.append(True)
        zk = (z + k + 8) % 8
        part = lax.dot_general(
            proj[s, zk], grads[:, pl.ds(pl.multiple_of(zk * TOK, TOK), TOK)],
            (((1,), (1,)), ((), ())), preferred_element_type=F32,
        )
        plan.spend(0.3)
        done[s] += 1
        if done[s] == 1:
            acc[s] = part
        elif done[s] < 8:
            acc[s] += part
        else:
            low[s, :, :COLS] = (acc[s] + part).astype(BF16)
            over_dp(s)

    def over_dp(s):
        if DP_PAIR[s]:
            for dy in ORDER:
                rows = pl.ds(pl.multiple_of(((1 - xl) * 8 + (y + dy) % 8) * R, R), R)
                m = send(s, low.at[s, rows], lowx.at[s, dy], DPX + dy, dp_at(1, 0), [("xlo", 1)], 16)
                plan.when([m], lambda dy=dy: over_y(s, dy))
            return
        messages = []
        offsets = [(dx, dy) for dx in range(2) for dy in range(8) if (dx, dy) != (0, 0)]
        for dx, dy in sorted(offsets, key=lambda o: (-min(o[1], 8 - o[1]), -o[0])):
            n = dx * 8 + dy
            device = dp_at(dx, dy)
            rows = pl.ds(pl.multiple_of(device[0] * R, R), R)
            messages.append((n, send(s, low.at[s, rows], lowr.at[s, n], DPX + n, device, ypath(dy), 16)))
        plan.when([m for _, m in messages], lambda: adam(s, [n for n, _ in messages]))

    def ypath(dy):
        return [("y+", dy)] if dy < 4 else [("y-", 8 - dy)] if dy > 4 else [("y+", 2), ("y-", 2)]

    pairs = {0: [], 1: []}

    def over_y(s, dy):
        rows = pl.ds(pl.multiple_of((xl * 8 + (y + dy) % 8) * R, R), R)
        low[s, rows, :] = (low[s, rows, :].astype(F32) + lowx[s, dy].astype(F32)).astype(BF16)
        plan.spend(0.04)
        if dy:
            n = 8 + dy
            pairs[s].append(send(s, low.at[s, rows], lowr.at[s, n], DPX + n, dp_at(0, dy), ypath(dy), 16))
        else:
            plan.when(pairs[s], lambda: adam(s, [8 + k for k in ORDER[:7]]))

    def adam(s, numbers):
        if "adam" not in need:
            need["adam"] = 1
            loads[3].wait()
            loads[4].wait()
        total = low[s, pl.ds(pl.multiple_of(dp * R, R), R), :COLS].astype(F32)
        for n in numbers:
            total = total + lowr[s, n, :, :COLS].astype(F32)
        rows = slice(s * R, s * R + R)
        m = 0.9 * moment[rows] + 0.1 * total
        v = 0.95 * second[rows] + 0.05 * total * total
        moment_new[rows] = m
        second_new[rows] = v
        step[s, :, :COLS] = (m / (jnp.sqrt(v) + 1e-8)).astype(BF16)
        plan.spend(0.3)

        for q in range(2):
            turn(s, q, xl).start()
        plan.when([], lambda: turned(s), ready=plan.now + 5.5)

    def turn(s, q, origin):
        place = pl.ds(pl.multiple_of(y * R, R), R)
        return pltpu.make_async_remote_copy(
            src_ref=step.at[s], dst_ref=steps.at[c, s, xl, place], send_sem=ss.at[s * COUNT + TRAN + q],
            recv_sem=rs.at[s * COUNT + TRAN + origin],
            device_id=(z * 2 + h, ((y - z - h + 12) % 8) * 4 + q * 2 + c), device_id_type=MESH,
        )

    def turned(s):
        for q in range(2):
            turn(s, q, q).wait_recv()
        spread(s)

    def srows(s, k, half=None):
        place = pl.ds(pl.multiple_of(((z + k + dp // 2 + dp % 2 + 12) % 8) * R, R), R)
        if half is None:
            return steps.at[c, s, :, place]
        return steps.at[c, s, half, place]

    def spread(s):
        def hand(number, k, half=None):
            ref = srows(s, k, half)
            m = send(s, ref, ref, SHST + number, at(dc=1), None, 32)
            plan.when([m], lambda: counted(("other", s), 9, lambda: finished(s, "other")))
            if number:
                counted(("this", s), 8, lambda: finished(s, "this"))

        def pass_on(number, k, dz, action, half=None):
            ref = srows(s, k, half)
            link = zlink(0 if dz < 0 else 1)
            m = send(s, ref, ref, STEP + number, at(dz), [(link, abs(dz))], 32 if half is None else 16)
            plan.when([m], action)

        def from_above():
            pass_on(4, 2, -2, lambda: hand(7, 4, 0), 0)
            pass_on(6, 2, -1, lambda: hand(5, 3))
            hand(1, 2)

        def from_below():
            pass_on(5, -2, 2, lambda: hand(8, 4, 1), 1)
            pass_on(7, -2, 1, lambda: hand(6, -3))
            hand(2, -2)

        pass_on(0, 0, -2, from_above)
        pass_on(1, 0, 2, from_below)
        pass_on(2, 0, -1, lambda: hand(3, 1))
        pass_on(3, 0, 1, lambda: hand(4, -1))
        hand(0, 0)

    def natural():
        low[:, :, 384:] = jnp.zeros((2, 2 * KEPT, 128), BF16)
        step[:, :, 384:] = jnp.zeros((2, R, 128), BF16)
        for s in range(2):
            both = [lhs[s, jnp.where(c == core, 1, 0)] for core in range(2)]
            feats[s] = jnp.concatenate(both, axis=0).T

    ends = []

    def finished(s, which):
        columns = c if which == "this" else 1 - c
        value = jnp.dot(feats[s], steps[columns, s].reshape(256, WIDE)[:, :COLS], preferred_element_type=F32)
        if which not in ends:
            wide[columns] = value
        else:
            wide[columns] += value
        plan.spend(0.2)
        ends.append(which)
        if len(ends) == 4:
            for half in range(2):
                dense[:, half * COLS : half * COLS + COLS] = wide[half].astype(BF16)

    exchange(1, 0)
    plan.when([], lambda: exchange(0, 0), ready=plan.now)
    plan.when([], lambda: exchange(1, 1), ready=plan.now + 0.01)
    plan.when([], lambda: exchange(0, 1), ready=plan.now + 0.02)
    plan.when([], natural, ready=plan.now + 5)
    for load in loads[2:]:
        load.start()
    plan.run()
    for m in plan.sent:
        m.copy.wait_send()
    for s in range(2):
        for q in range(2):
            turn(s, q, 0).wait_send()


def store(a, b, c, a_out, b_out, c_out, sems):
    copies = [
        pltpu.make_async_copy(src, dst, sems.at[n])
        for n, (src, dst) in enumerate(((a, a_out), (b, b_out), (c, c_out)))
    ]
    for cp in copies:
        cp.start()
    for cp in copies:
        cp.wait()


def shards(acts, grads, basis, moment, second):
    vmem = pl.BlockSpec(memory_space=pltpu.VMEM)
    hbm = pl.BlockSpec(memory_space=pltpu.HBM)
    results = pl.pallas_call(
        kernel,
        out_shape=(pltpu.VMEM(moment.shape, F32), pltpu.VMEM(second.shape, F32), pltpu.VMEM((256, 896), BF16)),
        in_specs=[hbm] * 5,
        out_specs=(vmem, vmem, vmem),
        scratch_shapes=[
            pltpu.VMEM((256, 2048), BF16),
            pltpu.VMEM((256, 512), BF16),
            pltpu.VMEM((COLS, 2048), BF16),
            pltpu.VMEM((32, COLS), F32),
            pltpu.VMEM((32, COLS), F32),
            pltpu.VMEM((2, 2, KEPT, 256), BF16),
            pltpu.VMEM((2, 256, 256), BF16),
            pltpu.VMEM((2, 8, KEPT, TOK), F32),
            pltpu.VMEM((2, 8, KEPT, TOK), BF16),
            pltpu.VMEM((2, 8, KEPT, TOK), BF16),
            pltpu.VMEM((2, 14, Q, TOK), BF16),
            pltpu.VMEM((2, 14, Q, TOK), BF16),
            pltpu.VMEM((2, 2, Q, TOK), BF16),
            pltpu.VMEM((2, 2, Q, TOK), BF16),
            pltpu.VMEM((8, Q, TOK), BF16),
            pltpu.VMEM((8, Q, TOK), BF16),
            pltpu.VMEM((8, Q, TOK), F32),
            pltpu.VMEM((8, Q, TOK), BF16),
            pltpu.VMEM((8, Q, TOK), BF16),
            pltpu.VMEM((2, 8, 2 * KEPT, TOK), BF16),
            pltpu.VMEM((2, 2 * KEPT, COLS), F32),
            pltpu.VMEM((2, 2 * KEPT, WIDE), BF16),
            pltpu.VMEM((2, 16, R, WIDE), BF16),
            pltpu.VMEM((2, 8, R, WIDE), BF16),
            pltpu.VMEM((2, R, WIDE), BF16),
            pltpu.VMEM((2, 2, 2, 128, WIDE), BF16),
            pltpu.VMEM((2, 256, COLS), F32),
            pltpu.SemaphoreType.DMA((5,)),
            pltpu.SemaphoreType.DMA((2 * COUNT,)),
            pltpu.SemaphoreType.DMA((2 * COUNT,)),
        ],
        compiler_params=pltpu.CompilerParams(
            collective_id=0, has_side_effects=True, vmem_limit_bytes=32 * 2**20
        ),
    )(*(pltpu.with_memory_space_constraint(a, pltpu.HBM) for a in (acts, basis, grads.T, moment, second)))
    return pl.pallas_call(
        store,
        out_shape=tuple(jax.ShapeDtypeStruct(r.shape, r.dtype) for r in results),
        in_specs=[vmem] * 3,
        out_specs=(pl.BlockSpec(memory_space=pl.ANY),) * 3,
        scratch_shapes=[pltpu.SemaphoreType.DMA((3,))],
        compiler_params=pltpu.CompilerParams(vmem_limit_bytes=2**21),
    )(*(pltpu.with_memory_space_constraint(r, pltpu.VMEM) for r in results))


def solution(mesh):
    in_specs = (P("fsdp", "dp"), P("dp", "fsdp"), P("fsdp", None), P("dp", "fsdp"), P("dp", "fsdp"))
    out_specs = (P("dp", "fsdp"), P("dp", "fsdp"), P("fsdp", "dp"))
    return jax.shard_map(shards, mesh=mesh, in_specs=in_specs, out_specs=out_specs, check_vma=False)
```

```python
import heapq

import jax
import jax.numpy as jnp
from jax import lax
from jax.experimental import pallas as pl
from jax.experimental.pallas import tpu as pltpu
from jax.sharding import PartitionSpec as P

F32 = jnp.float32
BF16 = jnp.bfloat16
MESH = pl.DeviceIdType.MESH
TOK = 256
KEPT = 128
Q = 64
COLS = 448
WIDE = 512
R = 16
DP_PAIR = (True, True)
ORDER = (4, 3, 5, 2, 6, 1, 7, 0)

CORE = 0
RING = 2
XHI = 16
GATH = 18
SHARE = 32
DPX = 40
TRAN = 56
STEP = 58
SHST = 66
RELAY = 75
COUNT = 84


class Message:
    def __init__(self, copy, arrival):
        self.copy, self.arrival = copy, arrival


class Plan:
    def __init__(self):
        self.now, self.heap, self.count, self.free = 0.0, [], 0, {}
        self.sent = []

    def spend(self, cost):
        self.now += cost

    def arrive(self, copy, path, kib):
        message = Message(copy, self.arrival(path, kib))
        self.sent.append(message)
        return message

    def arrival(self, path, kib):
        if path is None:
            return self.now + 0.85 + kib / 1000
        each = kib * 0.0227
        start = max([self.now] + [self.free.get(link, 0.0) for link, _ in path])
        for link, hops in path:
            self.free[link] = max(self.free.get(link, 0.0), self.now) + each * hops
        self.spend(0.03)
        return start + each + 2.6 + 0.6 * sum(hops for _, hops in path)

    def when(self, messages, action, ready=0.0):
        ready = max([ready] + [m.arrival for m in messages])
        heapq.heappush(self.heap, (ready, self.count, messages, action))
        self.count += 1

    def run(self):
        while self.heap:
            ready, _, messages, action = heapq.heappop(self.heap)
            while self.sent and self.sent[0].arrival < self.now - 1 and self.now + 0.2 < ready:
                self.sent.pop(0).copy.wait_send()
                self.spend(0.05)
            self.now = max(self.now, ready)
            for m in messages:
                m.copy.wait_recv()
            action()


def kernel(
    acts_hbm, basis_hbm, grads_hbm, moment_hbm, second_hbm,
    moment_new, second_new, dense,
    acts, basis, grads, moment, second,
    lhs, feats, own, csend, crecv, rsend, rrecv, xsend, xrecv, psend, precv, pown, fsend, frecv, proj, acc, low, lowr, lowx, step, steps, wide,
    local_sem, ss, rs,
):
    dp, fs = lax.axis_index("dp"), lax.axis_index("fsdp")
    xl, y = dp // 8, dp % 8
    z, h, c = fs // 4, (fs // 2) % 2, fs % 2

    def at(dz=0, dh=0, dc=0):
        return (dp, ((z + dz + 8) % 8) * 4 + ((h + dh) % 2) * 2 + (c + dc) % 2)

    def dp_at(dx, dy):
        return (((xl + dx) % 2) * 8 + (y + dy) % 8, fs)

    plan = Plan()

    def send(s, src, dst, number, device, path, kib):
        cp = pltpu.make_async_remote_copy(
            src_ref=src, dst_ref=dst, send_sem=ss.at[s * COUNT + number], recv_sem=rs.at[s * COUNT + number],
            device_id=device, device_id_type=MESH,
        )
        cp.start()
        return plan.arrive(cp, path, kib)

    loads = []
    for n, (src, dst) in enumerate((
        (basis_hbm, basis), (acts_hbm, acts), (grads_hbm, grads), (moment_hbm, moment), (second_hbm, second),
    )):
        loads.append(pltpu.make_async_copy(src, dst, local_sem.at[n]))
    loads[0].start()
    loads[1].start()

    barrier = pltpu.get_barrier_semaphore()
    greet = [at(dc=1), at(dh=1), at(1), at(-1), at(2), at(-2)]
    greet += [dp_at(1, 0)] + [dp_at(0, dy) for dy in range(1, 8)]
    for device in greet:
        pl.semaphore_signal(barrier, inc=1, device_id=device, device_id_type=MESH)
    loads[0].wait()
    for j in range(4):
        block = basis[:, j * 128 : j * 128 + 128].T
        place = jnp.where(c == j // 2, 1, 0)
        for b in range(4):
            for s in range(2):
                row = ((j % 2) * 4 + b) * R
                lhs[s, place, row : row + R] = block[b * 32 + s * R : b * 32 + s * R + R]
    loads[1].wait()

    def rows_of(half):
        return slice(half * Q, half * Q + Q)

    def slot(direction, half, hop):
        return direction * 7 + (0 if hop == 0 else 1 + (hop - 1) * 2 + half)

    def zlink(direction):
        return "z-" if direction == 0 else "z+"

    def partial(n):
        k = ORDER[n]
        tok = pl.ds(pl.multiple_of(((z + k) % 8) * TOK, TOK), TOK)
        product = jnp.dot(lhs[...].reshape(4 * KEPT, 256), acts[:, tok], preferred_element_type=F32)
        for s in range(2):
            csend[s, n] = product[s * 2 * KEPT : s * 2 * KEPT + KEPT].astype(BF16)
            own[s, n] = product[s * 2 * KEPT + KEPT : s * 2 * KEPT + 2 * KEPT]
        plan.spend(0.25)

    def exchange(part):
        first, last = ((0, 3), (3, 8))[part]
        for n in range(first, last):
            partial(n)
        if part == 0:
            pl.semaphore_wait(barrier, 14)
        place = pl.ds(first, last - first)
        for s in (1, 0):
            m = send(s, csend.at[s, place], crecv.at[s, place], CORE + part, at(dc=1), None, 64 * (last - first))
            plan.when([m], lambda s=s: ((pair_first, pair_rest), (reduce_start, reduce_rest))[s][part](s))

    def added(s, k, half):
        n = ORDER.index(k % 8)
        return own[s, n, rows_of(half), :] + crecv[s, n, rows_of(half), :].astype(F32)

    waiting = {}

    def ring_send(s, direction, half, hop, value):
        n = slot(direction, half, hop)
        rsend[s, n] = value.astype(BF16)
        plan.spend(0.08)
        hops = 2 if hop == 0 else 1
        sign = -1 if direction == 0 else 1
        m = send(s, rsend.at[s, n], rrecv.at[s, n], RING + n, at(sign * hops), [(zlink(direction), hops)], 32)
        if hop == 0:
            waiting[s, direction, half] = m
        else:
            plan.when([m], lambda: ring_next(s, direction, half, hop))

    def reduce_start(s):
        for direction in range(2):
            ring_send(s, direction, direction, 0, added(s, 4, direction))
        for half in range(2):
            for direction in range(2):
                k = 5 if direction == 0 else 3
                ring_send(s, direction, half ^ direction ^ 1, 1, added(s, k, half ^ direction ^ 1))

    ready = {0: False, 1: False}
    held = {0: [], 1: []}

    def reduce_rest(s):
        ready[s] = True
        for action in held[s]:
            action()

    sums = {}

    def ring_next(s, direction, half, hop):
        if not ready[s]:
            held[s].append(lambda: ring_next(s, direction, half, hop))
            return
        arrived = rrecv[s, slot(direction, half, hop)].astype(F32)
        if hop == 1 and half == direction:
            m = waiting[s, direction, half]
            m.copy.wait_recv()
            plan.now = max(plan.now, m.arrival)
            arrived = arrived + rrecv[s, slot(direction, half, 0)].astype(F32)
        if hop < 3:
            k = hop - 3 if direction == 0 else 3 - hop
            ring_send(s, direction, half, hop + 1, added(s, k, half) + arrived)
            return
        sums.setdefault((s, half), []).append(direction)
        if len(sums[s, half]) == 2:
            total = added(s, 0, half)
            for d in range(2):
                total = total + rrecv[s, slot(d, half, 3)].astype(F32)
            xsend[s, half] = total.astype(BF16)
            plan.spend(0.1)
            m = send(s, xsend.at[s, half], xrecv.at[s, half], XHI + half, at(dh=1), [("x", 1), ("x2", 1)], 32)
            plan.when([m], lambda: gather_start(s, half))

    mine = pl.multiple_of(h * Q, Q)
    theirs = pl.multiple_of((1 - h) * Q, Q)

    def pair(s, part):
        first, last = ((0, 3), (3, 8))[part]
        for n in range(first, last):
            for rows, out in ((theirs, None), (mine, own)):
                rows = pl.ds(rows, Q)
                value = own[s, n, rows, :] + crecv[s, n, rows, :].astype(F32)
                if out is None:
                    psend[n] = value.astype(BF16)
                else:
                    pown[n] = value
            plan.spend(0.1)
        place = pl.ds(first, last - first)
        m = send(
            s, psend.at[place], precv.at[place], XHI + part, at(dh=1), [("x", 1), ("x2", 1)], 32 * (last - first)
        )
        plan.when([m], lambda: (paired_first, paired_rest)[part](s))

    def pair_first(s):
        pair(s, 0)

    def pair_rest(s):
        pair(s, 1)

    def paired(k):
        n = ORDER.index(k % 8)
        return pown[n] + precv[n].astype(F32)

    def pair_send(s, n, direction, hops, value, action):
        rows = slice(0, value.shape[0])
        fsend[n, rows, :] = value.astype(BF16)
        plan.spend(0.05)
        sign = -1 if direction == 0 else 1
        m = send(
            s, fsend.at[n, rows], frecv.at[n, rows], RING + n, at(sign * hops), [(zlink(direction), hops)],
            value.shape[0] // 2,
        )
        plan.when([m], action)

    need = {}

    def counted(key, limit, action):
        need[key] = need.get(key, 0) + 1
        if need[key] == limit:
            action()

    def paired_first(s):
        for direction in range(2):
            value = paired(4)[direction * 32 : direction * 32 + 32]
            pair_send(s, direction * 4, direction, 2, value, lambda d=direction: pair_collect(s, d))
        for direction in range(2):
            value = paired(-3 if direction == 0 else 3)
            pair_send(s, direction * 4 + 1, direction, 1, value, lambda d=direction: pair_collect(s, d))

    def paired_rest(s):
        for direction in range(2):
            value = paired(-1 if direction == 0 else 1)
            pair_send(s, direction * 4 + 2, direction, 1, value, lambda: pair_total(s))
        for direction in range(2):
            pair_collect(s, direction)

    def pair_collect(s, direction):
        def collected():
            n = direction * 4
            value = paired(-2 if direction == 0 else 2) + frecv[n + 1].astype(F32)
            half = frecv[n, 0:32, :].astype(F32)
            zero = jnp.zeros_like(half)
            value = value + jnp.concatenate([half, zero] if direction == 0 else [zero, half], axis=0)
            pair_send(s, n + 3, direction, 2, value, lambda: pair_total(s))

        counted(("collect", direction), 3, collected)

    def pair_total(s):
        def totalled():
            value = paired(0)
            for n in (2, 3, 6, 7):
                value = value + frecv[n].astype(F32)
            proj[s, z, pl.ds(pl.multiple_of(c * KEPT + h * Q, Q), Q), :] = value.astype(BF16)
            plan.spend(0.1)
            pair_gather(s)

        counted("total", 4, totalled)

    def fpiece(s, k, half=None):
        row = c * KEPT + h * Q + (0 if half is None else half * 32)
        rows = pl.ds(pl.multiple_of(row, 32), Q if half is None else 32)
        return proj.at[s, (z + k + 8) % 8, rows]

    def pair_gather(s):
        def relay(k):
            ref = fpiece(s, k)
            m = send(s, ref, ref, RELAY + k % 8, at(dh=1), [("x", 1), ("x2", 1)], 32)
            plan.when([m], lambda: arrived_piece(s, k))
            arrived_piece(s, k)

        def pass_on(number, k, dz, action, half=None):
            ref = fpiece(s, k, half)
            link = zlink(0 if dz < 0 else 1)
            m = send(s, ref, ref, GATH + number, at(dz), [(link, abs(dz))], 32 if half is None else 16)
            plan.when([m], action)

        def cross(number, k, dz, action, half=None):
            ref = fpiece(s, k, half)
            path = [(zlink(0 if dz < 0 else 1), abs(dz)), ("x", 1), ("x2", 1)]
            m = send(s, ref, ref, RELAY + number, at(dz, dh=1), path, 32 if half is None else 16)
            plan.when([m], action)

        def farthest():
            counted("farthest", 2, lambda: arrived_piece(s, 4))

        def crossed():
            counted("crossed", 2, lambda: arrived_piece(s, 4))

        def from_above():
            pass_on(4, 2, -2, farthest, 0)
            cross(4, 2, -2, crossed, 0)
            pass_on(6, 2, -1, lambda: arrived_piece(s, 3))
            cross(3, 2, -1, lambda: arrived_piece(s, 3))
            relay(2)

        def from_below():
            pass_on(5, -2, 2, farthest, 1)
            cross(8, -2, 2, crossed, 1)
            pass_on(7, -2, 1, lambda: arrived_piece(s, -3))
            cross(5, -2, 1, lambda: arrived_piece(s, -3))
            relay(-2)

        pass_on(0, 0, -2, from_above)
        pass_on(1, 0, 2, from_below)
        pass_on(2, 0, -1, lambda: relay(1))
        pass_on(3, 0, 1, lambda: relay(-1))
        relay(0)

    def piece(s, k, half):
        return proj.at[s, (z + k + 8) % 8, pl.ds(pl.multiple_of(c * KEPT + half * Q, Q), Q)]

    def gath_send(s, direction, half, hop, k, hops=1):
        sign = -1 if direction == 0 else 1
        ref = piece(s, k, half)
        n = slot(direction, half, 3 - hop) if hops == 1 else slot(direction, half, 0)
        m = send(s, ref, ref, GATH + n, at(sign * hops), [(zlink(direction), hops)], 32)
        plan.when([m], lambda: gathered(s, direction, half, hop + hops))

    have = {}

    def arrived_piece(s, k):
        have[s, k] = have.get((s, k), 0) + 1
        if have[s, k] == 2:
            ref = proj.at[s, (z + k + 8) % 8, pl.ds(pl.multiple_of(c * KEPT, KEPT), KEPT)]
            m = send(s, ref, ref, SHARE + k % 8, at(dc=1), None, 64)
            plan.when([m], lambda: multiply(s, k))

    def gather_start(s, half):
        total = xsend[s, half].astype(F32) + xrecv[s, half].astype(F32)
        proj[s, z, pl.ds(pl.multiple_of(c * KEPT + half * Q, Q), Q), :] = total.astype(BF16)
        plan.spend(0.1)
        for direction in range(2):
            gath_send(s, direction, half, 0, 0)
        arrived_piece(s, 0)

    def gathered(s, direction, half, hop):
        sign = 1 if direction == 0 else -1
        if hop == 2 and half == direction:
            gath_send(s, direction, half, 2, sign * 2, hops=2)
        if hop < 3:
            gath_send(s, direction, half, hop, sign * hop)
        arrived_piece(s, sign * hop if hop < 4 else 4)

    loaded = []
    done = {0: 0, 1: 0}

    def multiply(s, k):
        if not loaded:
            loads[2].wait()
            loaded.append(True)
        zk = (z + k + 8) % 8
        part = lax.dot_general(
            proj[s, zk], grads[:, pl.ds(pl.multiple_of(zk * TOK, TOK), TOK)],
            (((1,), (1,)), ((), ())), preferred_element_type=F32,
        )
        plan.spend(0.3)
        done[s] += 1
        if done[s] == 1:
            acc[s] = part
        elif done[s] < 8:
            acc[s] += part
        else:
            low[s, :, :COLS] = (acc[s] + part).astype(BF16)
            over_dp(s)

    def over_dp(s):
        if DP_PAIR[s]:
            for dy in ORDER:
                rows = pl.ds(pl.multiple_of(((1 - xl) * 8 + (y + dy) % 8) * R, R), R)
                m = send(s, low.at[s, rows], lowx.at[s, dy], DPX + dy, dp_at(1, 0), [("xlo", 1)], 16)
                plan.when([m], lambda dy=dy: over_y(s, dy))
            return
        messages = []
        offsets = [(dx, dy) for dx in range(2) for dy in range(8) if (dx, dy) != (0, 0)]
        for dx, dy in sorted(offsets, key=lambda o: (-min(o[1], 8 - o[1]), -o[0])):
            n = dx * 8 + dy
            device = dp_at(dx, dy)
            rows = pl.ds(pl.multiple_of(device[0] * R, R), R)
            messages.append((n, send(s, low.at[s, rows], lowr.at[s, n], DPX + n, device, ypath(dy), 16)))
        plan.when([m for _, m in messages], lambda: adam(s, [n for n, _ in messages]))

    def ypath(dy):
        return [("y+", dy)] if dy < 4 else [("y-", 8 - dy)] if dy > 4 else [("y+", 2), ("y-", 2)]

    pairs = {0: [], 1: []}

    def over_y(s, dy):
        rows = pl.ds(pl.multiple_of((xl * 8 + (y + dy) % 8) * R, R), R)
        low[s, rows, :] = (low[s, rows, :].astype(F32) + lowx[s, dy].astype(F32)).astype(BF16)
        plan.spend(0.04)
        if dy:
            n = 8 + dy
            pairs[s].append(send(s, low.at[s, rows], lowr.at[s, n], DPX + n, dp_at(0, dy), ypath(dy), 16))
        else:
            plan.when(pairs[s], lambda: adam(s, [8 + k for k in ORDER[:7]]))

    def adam(s, numbers):
        if "adam" not in need:
            need["adam"] = 1
            loads[3].wait()
            loads[4].wait()
        total = low[s, pl.ds(pl.multiple_of(dp * R, R), R), :COLS].astype(F32)
        for n in numbers:
            total = total + lowr[s, n, :, :COLS].astype(F32)
        rows = slice(s * R, s * R + R)
        m = 0.9 * moment[rows] + 0.1 * total
        v = 0.95 * second[rows] + 0.05 * total * total
        moment_new[rows] = m
        second_new[rows] = v
        step[s, :, :COLS] = (m / (jnp.sqrt(v) + 1e-8)).astype(BF16)
        plan.spend(0.3)

        for q in range(2):
            turn(s, q, xl).start()
        plan.when([], lambda: turned(s), ready=plan.now + 5.5)

    def turn(s, q, origin):
        place = pl.ds(pl.multiple_of(y * R, R), R)
        return pltpu.make_async_remote_copy(
            src_ref=step.at[s], dst_ref=steps.at[c, s, xl, place], send_sem=ss.at[s * COUNT + TRAN + q],
            recv_sem=rs.at[s * COUNT + TRAN + origin],
            device_id=(z * 2 + h, ((y - z - h + 12) % 8) * 4 + q * 2 + c), device_id_type=MESH,
        )

    def turned(s):
        for q in range(2):
            turn(s, q, q).wait_recv()
        spread(s)

    def srows(s, k, half=None):
        place = pl.ds(pl.multiple_of(((z + k + dp // 2 + dp % 2 + 12) % 8) * R, R), R)
        if half is None:
            return steps.at[c, s, :, place]
        return steps.at[c, s, half, place]

    def spread(s):
        def hand(number, k, half=None):
            ref = srows(s, k, half)
            m = send(s, ref, ref, SHST + number, at(dc=1), None, 32)
            plan.when([m], lambda: counted(("other", s), 9, lambda: finished(s, "other")))
            if number:
                counted(("this", s), 8, lambda: finished(s, "this"))

        def pass_on(number, k, dz, action, half=None):
            ref = srows(s, k, half)
            link = zlink(0 if dz < 0 else 1)
            m = send(s, ref, ref, STEP + number, at(dz), [(link, abs(dz))], 32 if half is None else 16)
            plan.when([m], action)

        def from_above():
            pass_on(4, 2, -2, lambda: hand(7, 4, 0), 0)
            pass_on(6, 2, -1, lambda: hand(5, 3))
            hand(1, 2)

        def from_below():
            pass_on(5, -2, 2, lambda: hand(8, 4, 1), 1)
            pass_on(7, -2, 1, lambda: hand(6, -3))
            hand(2, -2)

        pass_on(0, 0, -2, from_above)
        pass_on(1, 0, 2, from_below)
        pass_on(2, 0, -1, lambda: hand(3, 1))
        pass_on(3, 0, 1, lambda: hand(4, -1))
        hand(0, 0)

    def natural():
        low[:, :, 384:] = jnp.zeros((2, 2 * KEPT, 128), BF16)
        step[:, :, 384:] = jnp.zeros((2, R, 128), BF16)
        for s in range(2):
            both = [lhs[s, jnp.where(c == core, 1, 0)] for core in range(2)]
            feats[s] = jnp.concatenate(both, axis=0).T

    ends = []

    def finished(s, which):
        columns = c if which == "this" else 1 - c
        value = jnp.dot(feats[s], steps[columns, s].reshape(256, WIDE)[:, :COLS], preferred_element_type=F32)
        if which not in ends:
            wide[columns] = value
        else:
            wide[columns] += value
        plan.spend(0.2)
        ends.append(which)
        if len(ends) == 4:
            for half in range(2):
                dense[:, half * COLS : half * COLS + COLS] = wide[half].astype(BF16)

    exchange(0)
    plan.when([], lambda: exchange(1), ready=plan.now)
    plan.when([], natural, ready=plan.now + 5)
    for load in loads[2:]:
        load.start()
    plan.run()
    for m in plan.sent:
        m.copy.wait_send()
    for s in range(2):
        for q in range(2):
            turn(s, q, 0).wait_send()


def store(a, b, c, a_out, b_out, c_out, sems):
    copies = [
        pltpu.make_async_copy(src, dst, sems.at[n])
        for n, (src, dst) in enumerate(((a, a_out), (b, b_out), (c, c_out)))
    ]
    for cp in copies:
        cp.start()
    for cp in copies:
        cp.wait()


def shards(acts, grads, basis, moment, second):
    vmem = pl.BlockSpec(memory_space=pltpu.VMEM)
    hbm = pl.BlockSpec(memory_space=pltpu.HBM)
    results = pl.pallas_call(
        kernel,
        out_shape=(pltpu.VMEM(moment.shape, F32), pltpu.VMEM(second.shape, F32), pltpu.VMEM((256, 896), BF16)),
        in_specs=[hbm] * 5,
        out_specs=(vmem, vmem, vmem),
        scratch_shapes=[
            pltpu.VMEM((256, 2048), BF16),
            pltpu.VMEM((256, 512), BF16),
            pltpu.VMEM((COLS, 2048), BF16),
            pltpu.VMEM((32, COLS), F32),
            pltpu.VMEM((32, COLS), F32),
            pltpu.VMEM((2, 2, KEPT, 256), BF16),
            pltpu.VMEM((2, 256, 256), BF16),
            pltpu.VMEM((2, 8, KEPT, TOK), F32),
            pltpu.VMEM((2, 8, KEPT, TOK), BF16),
            pltpu.VMEM((2, 8, KEPT, TOK), BF16),
            pltpu.VMEM((2, 14, Q, TOK), BF16),
            pltpu.VMEM((2, 14, Q, TOK), BF16),
            pltpu.VMEM((2, 2, Q, TOK), BF16),
            pltpu.VMEM((2, 2, Q, TOK), BF16),
            pltpu.VMEM((8, Q, TOK), BF16),
            pltpu.VMEM((8, Q, TOK), BF16),
            pltpu.VMEM((8, Q, TOK), F32),
            pltpu.VMEM((8, Q, TOK), BF16),
            pltpu.VMEM((8, Q, TOK), BF16),
            pltpu.VMEM((2, 8, 2 * KEPT, TOK), BF16),
            pltpu.VMEM((2, 2 * KEPT, COLS), F32),
            pltpu.VMEM((2, 2 * KEPT, WIDE), BF16),
            pltpu.VMEM((2, 16, R, WIDE), BF16),
            pltpu.VMEM((2, 8, R, WIDE), BF16),
            pltpu.VMEM((2, R, WIDE), BF16),
            pltpu.VMEM((2, 2, 2, 128, WIDE), BF16),
            pltpu.VMEM((2, 256, COLS), F32),
            pltpu.SemaphoreType.DMA((5,)),
            pltpu.SemaphoreType.DMA((2 * COUNT,)),
            pltpu.SemaphoreType.DMA((2 * COUNT,)),
        ],
        compiler_params=pltpu.CompilerParams(
            collective_id=0, has_side_effects=True, vmem_limit_bytes=32 * 2**20
        ),
    )(*(pltpu.with_memory_space_constraint(a, pltpu.HBM) for a in (acts, basis, grads.T, moment, second)))
    return pl.pallas_call(
        store,
        out_shape=tuple(jax.ShapeDtypeStruct(r.shape, r.dtype) for r in results),
        in_specs=[vmem] * 3,
        out_specs=(pl.BlockSpec(memory_space=pl.ANY),) * 3,
        scratch_shapes=[pltpu.SemaphoreType.DMA((3,))],
        compiler_params=pltpu.CompilerParams(vmem_limit_bytes=2**21),
    )(*(pltpu.with_memory_space_constraint(r, pltpu.VMEM) for r in results))


def solution(mesh):
    in_specs = (P("fsdp", "dp"), P("dp", "fsdp"), P("fsdp", None), P("dp", "fsdp"), P("dp", "fsdp"))
    out_specs = (P("dp", "fsdp"), P("dp", "fsdp"), P("fsdp", "dp"))
    return jax.shard_map(shards, mesh=mesh, in_specs=in_specs, out_specs=out_specs, check_vma=False)
```

```python
import heapq

import jax
import jax.numpy as jnp
from jax import lax
from jax.experimental import pallas as pl
from jax.experimental.pallas import tpu as pltpu
from jax.sharding import PartitionSpec as P

F32 = jnp.float32
BF16 = jnp.bfloat16
MESH = pl.DeviceIdType.MESH
TOK = 256
KEPT = 128
Q = 64
COLS = 448
WIDE = 512
R = 16
DP_PAIR = (True, True)
ORDER = (4, 3, 5, 2, 6, 1, 7, 0)

CORE = 0
RING = 2
XHI = 16
GATH = 18
SHARE = 32
DPX = 40
TRAN = 56
STEP = 58
SHST = 66
RELAY = 75
MORE = 84
COUNT = 86


class Message:
    def __init__(self, copy, arrival):
        self.copy, self.arrival = copy, arrival


class Plan:
    def __init__(self):
        self.now, self.heap, self.count, self.free = 0.0, [], 0, {}
        self.sent = []

    def spend(self, cost):
        self.now += cost

    def arrive(self, copy, path, kib):
        message = Message(copy, self.arrival(path, kib))
        self.sent.append(message)
        return message

    def arrival(self, path, kib):
        if path is None:
            return self.now + 0.85 + kib / 1000
        each = kib * 0.0227
        start = max([self.now] + [self.free.get(link, 0.0) for link, _ in path])
        for link, hops in path:
            self.free[link] = max(self.free.get(link, 0.0), self.now) + each * hops
        self.spend(0.03)
        return start + each + 2.6 + 0.6 * sum(hops for _, hops in path)

    def when(self, messages, action, ready=0.0):
        ready = max([ready] + [m.arrival for m in messages])
        heapq.heappush(self.heap, (ready, self.count, messages, action))
        self.count += 1

    def run(self):
        while self.heap:
            ready, _, messages, action = heapq.heappop(self.heap)
            while self.sent and self.sent[0].arrival < self.now - 1 and self.now + 0.2 < ready:
                self.sent.pop(0).copy.wait_send()
                self.spend(0.05)
            self.now = max(self.now, ready)
            for m in messages:
                m.copy.wait_recv()
            action()


def kernel(
    acts_hbm, basis_hbm, grads_hbm, moment_hbm, second_hbm,
    moment_new, second_new, dense,
    acts, basis, grads, moment, second,
    lhs, feats, own, csend, crecv, rsend, rrecv, xsend, xrecv, psend, precv, pown, fsend, frecv, proj, acc, low, lowr, lowx, step, steps, wide,
    local_sem, ss, rs,
):
    dp, fs = lax.axis_index("dp"), lax.axis_index("fsdp")
    xl, y = dp // 8, dp % 8
    z, h, c = fs // 4, (fs // 2) % 2, fs % 2

    def at(dz=0, dh=0, dc=0):
        return (dp, ((z + dz + 8) % 8) * 4 + ((h + dh) % 2) * 2 + (c + dc) % 2)

    def dp_at(dx, dy):
        return (((xl + dx) % 2) * 8 + (y + dy) % 8, fs)

    plan = Plan()

    def send(s, src, dst, number, device, path, kib):
        cp = pltpu.make_async_remote_copy(
            src_ref=src, dst_ref=dst, send_sem=ss.at[s * COUNT + number], recv_sem=rs.at[s * COUNT + number],
            device_id=device, device_id_type=MESH,
        )
        cp.start()
        return plan.arrive(cp, path, kib)

    loads = []
    for n, (src, dst) in enumerate((
        (basis_hbm, basis), (acts_hbm, acts), (grads_hbm, grads), (moment_hbm, moment), (second_hbm, second),
    )):
        loads.append(pltpu.make_async_copy(src, dst, local_sem.at[n]))
    loads[0].start()
    loads[1].start()

    barrier = pltpu.get_barrier_semaphore()
    greet = [at(dc=1), at(dh=1), at(1), at(-1), at(2), at(-2)]
    greet += [dp_at(1, 0)] + [dp_at(0, dy) for dy in range(1, 8)]
    for device in greet:
        pl.semaphore_signal(barrier, inc=1, device_id=device, device_id_type=MESH)
    loads[0].wait()
    for j in range(4):
        block = basis[:, j * 128 : j * 128 + 128].T
        place = jnp.where(c == j // 2, 1, 0)
        for b in range(4):
            for s in range(2):
                row = ((j % 2) * 4 + b) * R
                lhs[s, place, row : row + R] = block[b * 32 + s * R : b * 32 + s * R + R]
    loads[1].wait()

    def rows_of(half):
        return slice(half * Q, half * Q + Q)

    def slot(direction, half, hop):
        return direction * 7 + (0 if hop == 0 else 1 + (hop - 1) * 2 + half)

    def zlink(direction):
        return "z-" if direction == 0 else "z+"

    def partial(n):
        k = ORDER[n]
        tok = pl.ds(pl.multiple_of(((z + k) % 8) * TOK, TOK), TOK)
        product = jnp.dot(lhs[...].reshape(4 * KEPT, 256), acts[:, tok], preferred_element_type=F32)
        for s in range(2):
            csend[s, n] = product[s * 2 * KEPT : s * 2 * KEPT + KEPT].astype(BF16)
            own[s, n] = product[s * 2 * KEPT + KEPT : s * 2 * KEPT + 2 * KEPT]
        plan.spend(0.25)

    def exchange(part):
        first, last = ((0, 3), (3, 8))[part]
        for n in range(first, last):
            partial(n)
        if part == 0:
            pl.semaphore_wait(barrier, 14)
        place = pl.ds(first, last - first)
        for s in (1, 0):
            m = send(s, csend.at[s, place], crecv.at[s, place], CORE + part, at(dc=1), None, 64 * (last - first))
            plan.when([m], lambda s=s: ((pair_first, pair_rest), (reduce_start, reduce_rest))[s][part](s))

    def added(s, k, half):
        n = ORDER.index(k % 8)
        return own[s, n, rows_of(half), :] + crecv[s, n, rows_of(half), :].astype(F32)

    waiting = {}

    def ring_send(s, direction, half, hop, value):
        n = slot(direction, half, hop)
        rsend[s, n] = value.astype(BF16)
        plan.spend(0.08)
        hops = 2 if hop == 0 else 1
        sign = -1 if direction == 0 else 1
        m = send(s, rsend.at[s, n], rrecv.at[s, n], RING + n, at(sign * hops), [(zlink(direction), hops)], 32)
        if hop == 0:
            waiting[s, direction, half] = m
        else:
            plan.when([m], lambda: ring_next(s, direction, half, hop))

    def reduce_start(s):
        for direction in range(2):
            ring_send(s, direction, direction, 0, added(s, 4, direction))
        for half in range(2):
            for direction in range(2):
                k = 5 if direction == 0 else 3
                ring_send(s, direction, half ^ direction ^ 1, 1, added(s, k, half ^ direction ^ 1))

    ready = {0: False, 1: False}
    held = {0: [], 1: []}

    def reduce_rest(s):
        ready[s] = True
        for action in held[s]:
            action()

    sums = {}

    def ring_next(s, direction, half, hop):
        if not ready[s]:
            held[s].append(lambda: ring_next(s, direction, half, hop))
            return
        arrived = rrecv[s, slot(direction, half, hop)].astype(F32)
        if hop == 1 and half == direction:
            m = waiting[s, direction, half]
            m.copy.wait_recv()
            plan.now = max(plan.now, m.arrival)
            arrived = arrived + rrecv[s, slot(direction, half, 0)].astype(F32)
        if hop < 3:
            k = hop - 3 if direction == 0 else 3 - hop
            ring_send(s, direction, half, hop + 1, added(s, k, half) + arrived)
            return
        sums.setdefault((s, half), []).append(direction)
        if len(sums[s, half]) == 2:
            total = added(s, 0, half)
            for d in range(2):
                total = total + rrecv[s, slot(d, half, 3)].astype(F32)
            xsend[s, half] = total.astype(BF16)
            plan.spend(0.1)
            m = send(s, xsend.at[s, half], xrecv.at[s, half], XHI + half, at(dh=1), [("x", 1), ("x2", 1)], 32)
            plan.when([m], lambda: gather_start(s, half))

    mine = pl.multiple_of(h * Q, Q)
    theirs = pl.multiple_of((1 - h) * Q, Q)

    def pair(s, part):
        first, last = ((0, 3), (3, 8))[part]
        for n in range(first, last):
            for rows, out in ((theirs, None), (mine, own)):
                rows = pl.ds(rows, Q)
                value = own[s, n, rows, :] + crecv[s, n, rows, :].astype(F32)
                if out is None:
                    psend[n] = value.astype(BF16)
                else:
                    pown[n] = value
            plan.spend(0.1)
        place = pl.ds(first, last - first)
        m = send(
            s, psend.at[place], precv.at[place], XHI + part, at(dh=1), [("x", 1), ("x2", 1)], 32 * (last - first)
        )
        plan.when([m], lambda: (paired_first, paired_rest)[part](s))

    def pair_first(s):
        pair(s, 0)

    def pair_rest(s):
        pair(s, 1)

    def paired(k):
        n = ORDER.index(k % 8)
        return pown[n] + precv[n].astype(F32)

    def pair_send(s, n, direction, hops, value, action):
        rows = slice(0, value.shape[0])
        fsend[n, rows, :] = value.astype(BF16)
        plan.spend(0.05)
        sign = -1 if direction == 0 else 1
        m = send(
            s, fsend.at[n, rows], frecv.at[n, rows], RING + n, at(sign * hops), [(zlink(direction), hops)],
            value.shape[0] // 2,
        )
        plan.when([m], action)

    need = {}

    def counted(key, limit, action):
        need[key] = need.get(key, 0) + 1
        if need[key] == limit:
            action()

    def paired_first(s):
        for direction in range(2):
            value = paired(4)[direction * 32 : direction * 32 + 32]
            pair_send(s, direction * 4, direction, 2, value, lambda d=direction: pair_collect(s, d))
        for direction in range(2):
            value = paired(-3 if direction == 0 else 3)
            pair_send(s, direction * 4 + 1, direction, 1, value, lambda d=direction: pair_collect(s, d))

    def paired_rest(s):
        for direction in range(2):
            value = paired(-1 if direction == 0 else 1)
            pair_send(s, direction * 4 + 2, direction, 1, value, lambda: pair_total(s))
        for direction in range(2):
            pair_collect(s, direction)

    def pair_collect(s, direction):
        def collected():
            n = direction * 4
            value = paired(-2 if direction == 0 else 2) + frecv[n + 1].astype(F32)
            half = frecv[n, 0:32, :].astype(F32)
            zero = jnp.zeros_like(half)
            value = value + jnp.concatenate([half, zero] if direction == 0 else [zero, half], axis=0)
            pair_send(s, n + 3, direction, 2, value, lambda: pair_total(s))

        counted(("collect", direction), 3, collected)

    def pair_total(s):
        def totalled():
            value = paired(0)
            for n in (2, 3, 6, 7):
                value = value + frecv[n].astype(F32)
            proj[s, z, pl.ds(pl.multiple_of(c * KEPT + h * Q, Q), Q), :] = value.astype(BF16)
            plan.spend(0.1)
            pair_gather(s)

        counted("total", 4, totalled)

    def fpiece(s, k, half=None):
        row = c * KEPT + h * Q + (0 if half is None else half * 32)
        rows = pl.ds(pl.multiple_of(row, 32), Q if half is None else 32)
        return proj.at[s, (z + k + 8) % 8, rows]

    def pair_gather(s):
        def relay(k):
            ref = fpiece(s, k)
            m = send(s, ref, ref, RELAY + k % 8, at(dh=1), [("x", 1), ("x2", 1)], 32)
            plan.when([m], lambda: arrived_piece(s, k))
            arrived_piece(s, k)

        def pass_on(number, k, dz, action, half=None):
            ref = fpiece(s, k, half)
            link = zlink(0 if dz < 0 else 1)
            m = send(s, ref, ref, GATH + number, at(dz), [(link, abs(dz))], 32 if half is None else 16)
            plan.when([m], action)

        def cross(number, k, dz, action, half=None):
            ref = fpiece(s, k, half)
            path = [(zlink(0 if dz < 0 else 1), abs(dz)), ("x", 1), ("x2", 1)]
            m = send(s, ref, ref, RELAY + number, at(dz, dh=1), path, 32 if half is None else 16)
            plan.when([m], action)

        def farthest():
            counted("farthest", 2, lambda: arrived_piece(s, 4))

        def crossed():
            counted("crossed", 2, lambda: arrived_piece(s, 4))

        def from_above():
            pass_on(4, 2, -2, farthest, 0)
            cross(4, 2, -2, crossed, 0)
            pass_on(6, 2, -1, lambda: arrived_piece(s, 3))
            cross(3, 2, -1, lambda: arrived_piece(s, 3))
            relay(2)

        def from_below():
            pass_on(5, -2, 2, farthest, 1)
            cross(8, -2, 2, crossed, 1)
            pass_on(7, -2, 1, lambda: arrived_piece(s, -3))
            cross(5, -2, 1, lambda: arrived_piece(s, -3))
            relay(-2)

        pass_on(0, 0, -2, from_above)
        pass_on(1, 0, 2, from_below)
        pass_on(2, 0, -1, lambda: relay(1))
        pass_on(3, 0, 1, lambda: relay(-1))
        relay(0)

    def piece(s, k, half):
        return proj.at[s, (z + k + 8) % 8, pl.ds(pl.multiple_of(c * KEPT + half * Q, Q), Q)]

    def gath_send(s, direction, half, hop, k, hops=1):
        sign = -1 if direction == 0 else 1
        ref = piece(s, k, half)
        n = slot(direction, half, 3 - hop) if hops == 1 else slot(direction, half, 0)
        m = send(s, ref, ref, GATH + n, at(sign * hops), [(zlink(direction), hops)], 32)
        plan.when([m], lambda: gathered(s, direction, half, hop + hops))

    have = {}

    def arrived_piece(s, k):
        have[s, k] = have.get((s, k), 0) + 1
        if have[s, k] == 2:
            ref = proj.at[s, (z + k + 8) % 8, pl.ds(pl.multiple_of(c * KEPT, KEPT), KEPT)]
            m = send(s, ref, ref, SHARE + k % 8, at(dc=1), None, 64)
            plan.when([m], lambda: multiply(s, k))

    def gather_start(s, half):
        total = xsend[s, half].astype(F32) + xrecv[s, half].astype(F32)
        proj[s, z, pl.ds(pl.multiple_of(c * KEPT + half * Q, Q), Q), :] = total.astype(BF16)
        plan.spend(0.1)
        for direction in range(2):
            gath_send(s, direction, half, 0, 0)
        arrived_piece(s, 0)

    def gathered(s, direction, half, hop):
        sign = 1 if direction == 0 else -1
        if hop == 2 and half == direction:
            gath_send(s, direction, half, 2, sign * 2, hops=2)
        if hop < 3:
            gath_send(s, direction, half, hop, sign * hop)
        arrived_piece(s, sign * hop if hop < 4 else 4)

    loaded = []
    done = {0: 0, 1: 0}

    def multiply(s, k):
        if not loaded:
            loads[2].wait()
            loaded.append(True)
        zk = (z + k + 8) % 8
        part = lax.dot_general(
            proj[s, zk], grads[:, pl.ds(pl.multiple_of(zk * TOK, TOK), TOK)],
            (((1,), (1,)), ((), ())), preferred_element_type=F32,
        )
        plan.spend(0.3)
        done[s] += 1
        if done[s] == 1:
            acc[s] = part
        elif done[s] < 8:
            acc[s] += part
        else:
            low[s, :, :COLS] = (acc[s] + part).astype(BF16)
            over_dp(s)

    def over_dp(s):
        if DP_PAIR[s]:
            for dy in ORDER:
                rows = pl.ds(pl.multiple_of(((1 - xl) * 8 + (y + dy) % 8) * R, R), R)
                m = send(s, low.at[s, rows], lowx.at[s, dy], DPX + dy, dp_at(1, 0), [("xlo", 1)], 16)
                plan.when([m], lambda dy=dy: over_y(s, dy))
            return
        messages = []
        offsets = [(dx, dy) for dx in range(2) for dy in range(8) if (dx, dy) != (0, 0)]
        for dx, dy in sorted(offsets, key=lambda o: (-min(o[1], 8 - o[1]), -o[0])):
            n = dx * 8 + dy
            device = dp_at(dx, dy)
            rows = pl.ds(pl.multiple_of(device[0] * R, R), R)
            messages.append((n, send(s, low.at[s, rows], lowr.at[s, n], DPX + n, device, ypath(dy), 16)))
        plan.when([m for _, m in messages], lambda: adam(s, [n for n, _ in messages]))

    def ypath(dy):
        return [("y+", dy)] if dy < 4 else [("y-", 8 - dy)] if dy > 4 else [("y+", 2), ("y-", 2)]

    pairs = {0: [], 1: []}

    def over_y(s, dy):
        rows = pl.ds(pl.multiple_of((xl * 8 + (y + dy) % 8) * R, R), R)
        low[s, rows, :] = (low[s, rows, :].astype(F32) + lowx[s, dy].astype(F32)).astype(BF16)
        plan.spend(0.04)
        if dy:
            n = 8 + dy
            pairs[s].append(send(s, low.at[s, rows], lowr.at[s, n], DPX + n, dp_at(0, dy), ypath(dy), 16))
        else:
            plan.when(pairs[s], lambda: adam(s, [8 + k for k in ORDER[:7]]))

    def adam(s, numbers):
        if "adam" not in need:
            need["adam"] = 1
            loads[3].wait()
            loads[4].wait()
        total = low[s, pl.ds(pl.multiple_of(dp * R, R), R), :COLS].astype(F32)
        for n in numbers:
            total = total + lowr[s, n, :, :COLS].astype(F32)
        rows = slice(s * R, s * R + R)
        m = 0.9 * moment[rows] + 0.1 * total
        v = 0.95 * second[rows] + 0.05 * total * total
        moment_new[rows] = m
        second_new[rows] = v
        step[s, :, :COLS] = (m / (jnp.sqrt(v) + 1e-8)).astype(BF16)
        plan.spend(0.3)

        for q in range(2):
            turn(s, q, xl).start()
        plan.when([], lambda: turned(s), ready=plan.now + 5.5)

    def turn(s, q, origin):
        place = pl.ds(pl.multiple_of(y * R, R), R)
        return pltpu.make_async_remote_copy(
            src_ref=step.at[s], dst_ref=steps.at[c, s, xl, place], send_sem=ss.at[s * COUNT + TRAN + q],
            recv_sem=rs.at[s * COUNT + TRAN + origin],
            device_id=(z * 2 + h, ((y - z - h + 12) % 8) * 4 + q * 2 + c), device_id_type=MESH,
        )

    def turned(s):
        for q in range(2):
            turn(s, q, q).wait_recv()
        spread(s)

    def srows(s, k, half=None):
        place = pl.ds(pl.multiple_of(((z + k + dp // 2 + dp % 2 + 12) % 8) * R, R), R)
        if half is None:
            return steps.at[c, s, :, place]
        return steps.at[c, s, half, place]

    def spread(s):
        def hand(number, k, half=None):
            ref = srows(s, k, half)
            m = send(s, ref, ref, SHST + number, at(dc=1), None, 32)
            plan.when([m], lambda: counted(("other", s), 9, lambda: finished(s, "other")))
            if number:
                counted(("this", s), 8, lambda: finished(s, "this"))

        def pass_on(number, k, dz, action, half=None):
            ref = srows(s, k, half)
            link = zlink(0 if dz < 0 else 1)
            m = send(s, ref, ref, STEP + number, at(dz), [(link, abs(dz))], 32 if half is None else 16)
            plan.when([m], action)

        def from_above():
            pass_on(6, 2, -1, lambda: hand(5, 3))
            hand(1, 2)

        def from_below():
            pass_on(7, -2, 1, lambda: hand(6, -3))
            hand(2, -2)

        def half_above(first):
            if first:
                pass_on(4, 2, -2, lambda: hand(7, 4, 0), 0)
            counted(("above", s), 2, from_above)

        def half_below(first):
            if first:
                pass_on(5, -2, 2, lambda: hand(8, 4, 1), 1)
            counted(("below", s), 2, from_below)

        pass_on(0, 0, -2, lambda: half_above(True), 0)
        pass_on(1, 0, 2, lambda: half_below(True), 1)
        pass_on(MORE - STEP, 0, -2, lambda: half_above(False), 1)
        pass_on(MORE - STEP + 1, 0, 2, lambda: half_below(False), 0)
        pass_on(2, 0, -1, lambda: hand(3, 1))
        pass_on(3, 0, 1, lambda: hand(4, -1))
        hand(0, 0)

    def natural():
        low[:, :, 384:] = jnp.zeros((2, 2 * KEPT, 128), BF16)
        step[:, :, 384:] = jnp.zeros((2, R, 128), BF16)
        for s in range(2):
            both = [lhs[s, jnp.where(c == core, 1, 0)] for core in range(2)]
            feats[s] = jnp.concatenate(both, axis=0).T

    ends = []

    def finished(s, which):
        columns = c if which == "this" else 1 - c
        value = jnp.dot(feats[s], steps[columns, s].reshape(256, WIDE)[:, :COLS], preferred_element_type=F32)
        if which not in ends:
            wide[columns] = value
        else:
            wide[columns] += value
        plan.spend(0.2)
        ends.append(which)
        if len(ends) == 4:
            for half in range(2):
                dense[:, half * COLS : half * COLS + COLS] = wide[half].astype(BF16)

    exchange(0)
    plan.when([], lambda: exchange(1), ready=plan.now)
    plan.when([], natural, ready=plan.now + 5)
    for load in loads[2:]:
        load.start()
    plan.run()
    for m in plan.sent:
        m.copy.wait_send()
    for s in range(2):
        for q in range(2):
            turn(s, q, 0).wait_send()


def store(a, b, c, a_out, b_out, c_out, sems):
    copies = [
        pltpu.make_async_copy(src, dst, sems.at[n])
        for n, (src, dst) in enumerate(((a, a_out), (b, b_out), (c, c_out)))
    ]
    for cp in copies:
        cp.start()
    for cp in copies:
        cp.wait()


def shards(acts, grads, basis, moment, second):
    vmem = pl.BlockSpec(memory_space=pltpu.VMEM)
    hbm = pl.BlockSpec(memory_space=pltpu.HBM)
    results = pl.pallas_call(
        kernel,
        out_shape=(pltpu.VMEM(moment.shape, F32), pltpu.VMEM(second.shape, F32), pltpu.VMEM((256, 896), BF16)),
        in_specs=[hbm] * 5,
        out_specs=(vmem, vmem, vmem),
        scratch_shapes=[
            pltpu.VMEM((256, 2048), BF16),
            pltpu.VMEM((256, 512), BF16),
            pltpu.VMEM((COLS, 2048), BF16),
            pltpu.VMEM((32, COLS), F32),
            pltpu.VMEM((32, COLS), F32),
            pltpu.VMEM((2, 2, KEPT, 256), BF16),
            pltpu.VMEM((2, 256, 256), BF16),
            pltpu.VMEM((2, 8, KEPT, TOK), F32),
            pltpu.VMEM((2, 8, KEPT, TOK), BF16),
            pltpu.VMEM((2, 8, KEPT, TOK), BF16),
            pltpu.VMEM((2, 14, Q, TOK), BF16),
            pltpu.VMEM((2, 14, Q, TOK), BF16),
            pltpu.VMEM((2, 2, Q, TOK), BF16),
            pltpu.VMEM((2, 2, Q, TOK), BF16),
            pltpu.VMEM((8, Q, TOK), BF16),
            pltpu.VMEM((8, Q, TOK), BF16),
            pltpu.VMEM((8, Q, TOK), F32),
            pltpu.VMEM((8, Q, TOK), BF16),
            pltpu.VMEM((8, Q, TOK), BF16),
            pltpu.VMEM((2, 8, 2 * KEPT, TOK), BF16),
            pltpu.VMEM((2, 2 * KEPT, COLS), F32),
            pltpu.VMEM((2, 2 * KEPT, WIDE), BF16),
            pltpu.VMEM((2, 16, R, WIDE), BF16),
            pltpu.VMEM((2, 8, R, WIDE), BF16),
            pltpu.VMEM((2, R, WIDE), BF16),
            pltpu.VMEM((2, 2, 2, 128, WIDE), BF16),
            pltpu.VMEM((2, 256, COLS), F32),
            pltpu.SemaphoreType.DMA((5,)),
            pltpu.SemaphoreType.DMA((2 * COUNT,)),
            pltpu.SemaphoreType.DMA((2 * COUNT,)),
        ],
        compiler_params=pltpu.CompilerParams(
            collective_id=0, has_side_effects=True, vmem_limit_bytes=32 * 2**20
        ),
    )(*(pltpu.with_memory_space_constraint(a, pltpu.HBM) for a in (acts, basis, grads.T, moment, second)))
    return pl.pallas_call(
        store,
        out_shape=tuple(jax.ShapeDtypeStruct(r.shape, r.dtype) for r in results),
        in_specs=[vmem] * 3,
        out_specs=(pl.BlockSpec(memory_space=pl.ANY),) * 3,
        scratch_shapes=[pltpu.SemaphoreType.DMA((3,))],
        compiler_params=pltpu.CompilerParams(vmem_limit_bytes=2**21),
    )(*(pltpu.with_memory_space_constraint(r, pltpu.VMEM) for r in results))


def solution(mesh):
    in_specs = (P("fsdp", "dp"), P("dp", "fsdp"), P("fsdp", None), P("dp", "fsdp"), P("dp", "fsdp"))
    out_specs = (P("dp", "fsdp"), P("dp", "fsdp"), P("fsdp", "dp"))
    return jax.shard_map(shards, mesh=mesh, in_specs=in_specs, out_specs=out_specs, check_vma=False)
```
